512 devices in a mesh: img: 16 (over y, z_lo), txt: 32 (over z_hi, x, core).
Axes of the slice: x: 4, y: 4, z: 16 (z_hi: 4, z_lo: 4; z = z_hi * 4 + z_lo), core: 2. Of those that a mesh axis runs over, the one named last changes fastest.
Arguments:
- images: bfloat16 [16384, 1024], P(('img', 'txt')), may hold values from -2 to 2
- texts: bfloat16 [16, 1024, 1024], P('img', 'txt'), may hold values from -2 to 2
Outputs:
- contrastive_loss: float32 [], replicated
- grad_images: bfloat16 [16384, 1024], P(('img', 'txt'))
- grad_texts: bfloat16 [16, 1024, 1024], P('img', 'txt')
The draws below stay inside these ranges and needn't reach their ends.
All inputs are finite; a program needn't handle non-finite values.
Results may differ from the reference program's by a relative error of at most 0.02.
Values may be sent and summed in bfloat16 or wider, within the bound.
A program may use at most 64 MiB of HBM per device.

```python
import math
import jax
import jax.numpy as jnp
from jax import lax

D = 1024
ROWS_DEV = 32
PAIRS = 16384
IMG_BLOCK = 1024
TXT_BLOCK = 512
N_IMG = 16
N_TXT = 32


def rising_rows():
    return 0.6 + 1.2 * jnp.arange(PAIRS, dtype=jnp.float32) / (PAIRS - 1)


def draw_images(key, part):
    key = jax.random.fold_in(key, 3)
    key_noise, key_scale = jax.random.split(key, 2)
    spread = math.sqrt(0.07 / math.sqrt(D))
    rising = rising_rows()
    jitter = jnp.clip(jax.random.normal(key_noise, (PAIRS, D), jnp.float32), -4.0, 4.0)
    scales = jnp.exp(jax.random.uniform(key_scale, (PAIRS, 1), jnp.float32, math.log(0.25), math.log(2.5)))
    values = spread * jitter * scales * rising[:, None]
    return jnp.clip(values, -2.0, 2.0).astype(jnp.bfloat16)


def draw_texts(key, part):
    key = jax.random.fold_in(key, 5)
    key_noise, key_scale = jax.random.split(key, 2)
    spread = math.sqrt(0.07 / math.sqrt(D))
    rising = rising_rows()
    jitter = jnp.clip(jax.random.normal(key_noise, (PAIRS, D), jnp.float32), -4.0, 4.0)
    scales = jnp.exp(jax.random.uniform(key_scale, (PAIRS, 1), jnp.float32, math.log(0.25), math.log(2.5)))
    values = spread * jitter * scales * rising[:, None]
    values = jnp.clip(values, -2.0, 2.0)
    return values.reshape(N_TXT, N_IMG, ROWS_DEV, D).transpose(1, 0, 2, 3).reshape(N_IMG, N_TXT * ROWS_DEV, D).astype(jnp.bfloat16)


def setup_inputs(seed: int = 0) -> dict:
    streams_of = jax.random.split(jax.random.key(seed), 3)
    images = draw_images(jax.random.fold_in(streams_of[2], 71), 0)
    texts = draw_texts(jax.random.fold_in(streams_of[2], 71), 0)
    return {"images": images, "texts": texts}


LOGIT_SCALE = 1.0 / 0.07


def order_texts(texts):
    return texts.reshape(N_IMG, N_TXT, ROWS_DEV, D).transpose(1, 0, 2, 3).reshape(PAIRS, D)


def block_logits(img_block, text_rows):
    return LOGIT_SCALE * jnp.dot(img_block, text_rows.T, preferred_element_type=jnp.float32)


def reference(images, texts):
    text_rows = order_texts(texts)
    img_blocks = images.reshape(N_IMG, IMG_BLOCK, D)
    starts = jnp.arange(N_IMG, dtype=jnp.int32) * IMG_BLOCK

    def forward(state, img_block):
        col_peak, col_total = state
        logits = block_logits(img_block, text_rows)
        row_peak = jnp.max(logits, axis=1)
        row_lse = row_peak + jnp.log(jnp.sum(jnp.exp(logits - row_peak[:, None]), axis=1))
        new_peak = jnp.maximum(col_peak, jnp.max(logits, axis=0))
        col_total = col_total * jnp.exp(col_peak - new_peak) + jnp.sum(jnp.exp(logits - new_peak[None, :]), axis=0)
        return (new_peak, col_total), row_lse

    start_state = (jnp.full((PAIRS,), -jnp.inf, jnp.float32), jnp.zeros((PAIRS,), jnp.float32))
    (col_peak, col_total), row_lse = lax.scan(forward, start_state, img_blocks)
    col_lse = col_peak + jnp.log(col_total)
    positive = LOGIT_SCALE * jnp.sum(images.astype(jnp.float32) * text_rows.astype(jnp.float32), axis=1)
    contrastive_loss = (jnp.sum(row_lse) + jnp.sum(col_lse) - 2.0 * jnp.sum(positive)) / (2.0 * PAIRS)
    text_blocks = text_rows.reshape(N_TXT, TXT_BLOCK, D).astype(jnp.float32)

    def backward(text_total, inputs):
        img_block, start_row, block_lse = inputs
        logits = block_logits(img_block, text_rows)
        row_ids = start_row + jnp.arange(IMG_BLOCK, dtype=jnp.int32)[:, None]
        col_ids = jnp.arange(PAIRS, dtype=jnp.int32)[None, :]
        diagonal = (row_ids == col_ids).astype(jnp.float32)
        weights = (0.5 * LOGIT_SCALE * (jnp.exp(logits - block_lse[:, None]) + jnp.exp(logits - col_lse[None, :]) - 2.0 * diagonal)).astype(jnp.bfloat16)
        partials = jnp.einsum("rjc,jcd->jrd", weights.reshape(IMG_BLOCK, N_TXT, TXT_BLOCK).astype(jnp.float32), text_blocks, precision=lax.Precision.HIGHEST)
        rounded = lax.optimization_barrier(partials.astype(jnp.bfloat16))
        grad_block = jnp.sum(rounded.astype(jnp.float32), axis=0).astype(jnp.bfloat16)
        text_part = jnp.dot(weights.T, img_block, preferred_element_type=jnp.float32)
        text_part = lax.optimization_barrier(text_part.astype(jnp.bfloat16))
        return text_total + text_part.astype(jnp.float32), grad_block

    text_total, grad_blocks = lax.scan(backward, jnp.zeros((PAIRS, D), jnp.float32), (img_blocks, starts, row_lse))
    grad_images = grad_blocks.reshape(PAIRS, D)
    grad_texts = text_total.astype(jnp.bfloat16).reshape(N_TXT, N_IMG, ROWS_DEV, D).transpose(1, 0, 2, 3).reshape(N_IMG, N_TXT * ROWS_DEV, D)
    return (contrastive_loss, grad_images, grad_texts)
```

```python
import jax
import jax.numpy as jnp
from jax import lax
from jax.experimental import pallas as pl
from jax.experimental.pallas import tpu as pltpu
from jax.sharding import PartitionSpec as P

LOGIT_SCALE = 1.0 / 0.07
MESH = pl.DeviceIdType.MESH
F32 = jnp.float32
BF16 = jnp.bfloat16

N = 4
CORES = 2
ROWS = 32
HALF = ROWS // 2
D = 1024
CHUNK = N * CORES * ROWS
COLS = N * N * ROWS
PAIRS = N * CHUNK * N * N
STRIP = 64


def dma(shape):
    return pltpu.SemaphoreType.DMA(shape)


SCRATCH = dict(
    image=pltpu.VMEM((N, N, CORES, ROWS, D), BF16),
    text=pltpu.VMEM((N, N, ROWS, D), BF16),
    row_exp=pltpu.VMEM((N, CHUNK, COLS), F32),
    col_exp=pltpu.VMEM((N, CHUNK, COLS), F32),
    row_peak=pltpu.VMEM((N, CHUNK, 128), F32),
    row_scale=pltpu.VMEM((N, CHUNK, 128), F32),
    row_log=pltpu.VMEM((CHUNK, 128), F32),
    row_dense=pltpu.VMEM((N, 8, 128), F32),
    col_peak=pltpu.VMEM((N, 8, COLS), F32),
    col_log=pltpu.VMEM((N, 8, COLS), F32),
    diag=pltpu.VMEM((8, 128), F32),
    weights=pltpu.VMEM((N, CHUNK, COLS), BF16),
    part_image=pltpu.VMEM((N, N, CORES, ROWS, D), BF16),
    part_core=pltpu.VMEM((N, N, ROWS, D), BF16),
    xa=pltpu.VMEM((N, N, ROWS, D), BF16),
    xr1=pltpu.VMEM((N, 2, HALF, D), BF16),
    xb=pltpu.VMEM((N, 2, ROWS, D), BF16),
    xr2=pltpu.VMEM((N, 2, ROWS, D), BF16),
    za=pltpu.VMEM((N, ROWS, D), BF16),
    zr1=pltpu.VMEM((2, HALF, D), BF16),
    zb=pltpu.VMEM((2, ROWS, D), BF16),
    zr2=pltpu.VMEM((2, ROWS, D), BF16),
    part_text=pltpu.VMEM((N, N, ROWS, D), BF16),
    yr1=pltpu.VMEM((N, 2, HALF, D), BF16),
    yb=pltpu.VMEM((N, 2, ROWS, D), BF16),
    yr2=pltpu.VMEM((N, 2, ROWS, D), BF16),
    ta=pltpu.VMEM((N, ROWS, D), BF16),
    tr=pltpu.VMEM((N, ROWS, D), BF16),
    row1=pltpu.VMEM((N * CORES, 8, 128), F32),
    row2=pltpu.VMEM((N, 8, 128), F32),
    col1=pltpu.VMEM((N, 8, 128), F32),
    col2=pltpu.VMEM((N, 8, 128), F32),
    loss1=pltpu.VMEM((N * CORES, 8, 128), F32),
    loss2=pltpu.VMEM((N, 8, 128), F32),
    loss3=pltpu.VMEM((N, 8, 128), F32),
    loss4=pltpu.VMEM((N, 8, 128), F32),
    local_sem=dma((2,)),
    gz_s=dma((4,)), gz_r=dma((4,)),
    gx_s=dma((N, 4)), gx_r=dma((N, 4)),
    gc_s=dma((N,)), gc_r=dma((N,)),
    gl_s=dma((N,)), gl_r=dma((N,)),
    gy_s=dma((N, 4)), gy_r=dma((N, 4)),
    r1_s=dma((8,)), r1_r=dma((8,)),
    r2_s=dma((N,)), r2_r=dma((N,)),
    c1_s=dma((N,)), c1_r=dma((N,)),
    c2_s=dma((N,)), c2_r=dma((N,)),
    l1_s=dma((8,)), l1_r=dma((8,)),
    l2_s=dma((N,)), l2_r=dma((N,)),
    l3_s=dma((N,)), l3_r=dma((N,)),
    l4_s=dma((N,)), l4_r=dma((N,)),
    sc_s=dma((N,)), sc_r=dma((N,)),
    sx_s=dma((N, 4)), sx_r=dma((N, 4)),
    sz_s=dma((4,)), sz_r=dma((4,)),
    sy_s=dma((N, 4)), sy_r=dma((N, 4)),
    sl_s=dma((N,)), sl_r=dma((N,)),
)
NAMES = list(SCRATCH)


class Refs:
    def __init__(self, refs):
        for name, ref in zip(NAMES, refs):
            setattr(self, name, ref)


def log_sum(parts):
    peak = parts[0]
    for part in parts[1:]:
        peak = jnp.maximum(peak, part)
    total = jnp.exp(parts[0] - peak)
    for part in parts[1:]:
        total = total + jnp.exp(part - peak)
    return peak + jnp.log(total)


def eye():
    rows = lax.broadcasted_iota(jnp.int32, (128, 128), 0)
    cols = lax.broadcasted_iota(jnp.int32, (128, 128), 1)
    return rows == cols


def kernel(img_hbm, txt_hbm, loss_out, gi_out, gt_out, *refs):
    s = Refs(refs)
    img, txt = lax.axis_index("img"), lax.axis_index("txt")
    y, zl = img // N, lax.rem(img, N)
    zh, xc = txt // (N * CORES), lax.rem(txt, N * CORES)
    x, c = xc // CORES, lax.rem(xc, CORES)

    def up(place, by):
        return lax.rem(place + by, N)

    def at_x(place):
        return (img, (zh * N + place) * CORES + c)

    def at_xc(place):
        return (img, zh * (N * CORES) + place)

    def at_zh(place):
        return (img, place * (N * CORES) + xc)

    def at_y(place):
        return (place * N + zl, txt)

    def at_zl(place):
        return (y * N + place, txt)

    other_core = (img, (zh * N + x) * CORES + (1 - c))

    own_image = pltpu.make_async_copy(img_hbm, s.image.at[zh, x, c], s.local_sem.at[0])
    own_text = pltpu.make_async_copy(txt_hbm.at[0], s.text.at[y, zl], s.local_sem.at[1])
    own_image.start()
    own_text.start()

    barrier = pltpu.get_barrier_semaphore()
    partners = [at_xc(lax.rem(xc + by, N * CORES)) for by in range(1, N * CORES)]
    for by in range(1, N):
        partners += [at_zh(up(zh, by)), at_y(up(y, by)), at_zl(up(zl, by))]
    for partner in partners:
        pl.semaphore_signal(barrier, inc=1, device_id=partner, device_id_type=MESH)
    pl.semaphore_wait(barrier, len(partners))

    sent = []

    def remote(src, dst, send_sem, recv_sem, device):
        return pltpu.make_async_remote_copy(
            src_ref=src, dst_ref=dst, send_sem=send_sem, recv_sem=recv_sem,
            device_id=device, device_id_type=MESH,
        )

    def send(*args):
        copy = remote(*args)
        copy.start()
        sent.append(copy)

    def arrive(dst, send_sem, recv_sem, device):
        remote(dst, dst, send_sem, recv_sem, device).wait_recv()

    low, high = pl.ds(0, HALF), pl.ds(HALF, HALF)

    class Gather:
        def __init__(self, slot, me, device, ss, rs):
            self.slot, self.me, self.device, self.ss, self.rs = slot, me, device, ss, rs
            self.right, self.left, self.far = up(me, 1), up(me, 3), up(me, 2)

        def full(self):
            own = self.slot(self.me)
            send(own, own, self.ss(0), self.rs(0), self.device(self.right))
            send(own, own, self.ss(1), self.rs(1), self.device(self.left))

        def forward_left(self):
            block = self.slot(self.left)
            arrive(block, self.ss(0), self.rs(0), self.device(self.left))
            send(block.at[low], block.at[low], self.ss(2), self.rs(2), self.device(self.right))

        def forward_right(self):
            block = self.slot(self.right)
            arrive(block, self.ss(1), self.rs(1), self.device(self.right))
            send(block.at[high], block.at[high], self.ss(3), self.rs(3), self.device(self.left))

        def forward(self):
            self.forward_left()
            self.forward_right()

        def finish(self):
            block = self.slot(self.far)
            arrive(block.at[low], self.ss(2), self.rs(2), self.device(self.left))
            arrive(block.at[high], self.ss(3), self.rs(3), self.device(self.right))

    class Scatter:
        def __init__(self, slot, r1, b, r2, me, device, ss, rs):
            self.slot, self.r1, self.b, self.r2 = slot, r1, b, r2
            self.me, self.device, self.ss, self.rs = me, device, ss, rs
            self.right, self.left, self.far = up(me, 1), up(me, 3), up(me, 2)

        def first(self):
            block = self.slot(self.far)
            send(block.at[low], self.r1(0), self.ss(0), self.rs(0), self.device(self.right))
            send(block.at[high], self.r1(1), self.ss(1), self.rs(1), self.device(self.left))

        def second(self):
            block, out = self.slot(self.right), self.b(0)
            arrive(self.r1(0), self.ss(0), self.rs(0), self.device(self.left))
            out[low] = (block[low].astype(F32) + self.r1(0)[...].astype(F32)).astype(BF16)
            out[high] = block[high]
            send(out, self.r2(0), self.ss(2), self.rs(2), self.device(self.right))
            block, out = self.slot(self.left), self.b(1)
            arrive(self.r1(1), self.ss(1), self.rs(1), self.device(self.right))
            out[high] = (block[high].astype(F32) + self.r1(1)[...].astype(F32)).astype(BF16)
            out[low] = block[low]
            send(out, self.r2(1), self.ss(3), self.rs(3), self.device(self.left))

        def third(self):
            arrive(self.r2(0), self.ss(2), self.rs(2), self.device(self.left))
            arrive(self.r2(1), self.ss(3), self.rs(3), self.device(self.right))
            total = self.slot(self.me)[...].astype(F32) + self.r2(0)[...].astype(F32)
            return (total + self.r2(1)[...].astype(F32)).astype(BF16)

    def exchange(buf, me, count, device, ss, rs):
        for by in range(1, count):
            peer = lax.rem(me + by, count)
            send(buf.at[me], buf.at[me], ss.at[by], rs.at[by], device(peer))

    def collect(buf, me, count, device, ss, rs):
        for by in range(1, count):
            peer = lax.rem(me + count - by, count)
            arrive(buf.at[peer], ss.at[by], rs.at[by], device(peer))
        return [buf[j] for j in range(count)]

    gz = Gather(lambda o: s.image.at[o, x, c], zh, at_zh, lambda k: s.gz_s.at[k], lambda k: s.gz_r.at[k])
    gx = {
        by: Gather(
            lambda o, zo=up(zh, by): s.image.at[zo, o, c], x, at_x,
            lambda k, zo=up(zh, by): s.gx_s.at[zo, k], lambda k, zo=up(zh, by): s.gx_r.at[zo, k],
        )
        for by in range(N)
    }
    gy = {
        by: Gather(
            lambda o, zo=up(zl, by): s.text.at[o, zo], y, at_y,
            lambda k, zo=up(zl, by): s.gy_s.at[zo, k], lambda k, zo=up(zl, by): s.gy_r.at[zo, k],
        )
        for by in range(N)
    }
    own_image.wait()
    gz.full()
    own_text.wait()
    for by in (1, 3, 2):
        mine = s.text.at[y, zl]
        send(mine, mine, s.gl_s.at[by], s.gl_r.at[by], at_zl(up(zl, by)))
    gx[0].full()
    gy[0].full()
    gz.forward_left()
    gx[3].full()
    gz.forward_right()
    gx[1].full()
    for by in (1, 3, 2):
        peer = up(zl, N - by)
        arrive(s.text.at[y, peer], s.gl_s.at[by], s.gl_r.at[by], at_zl(peer))
        gy[N - by].full()
    gx[0].forward()
    gy[0].forward()
    gx[3].forward()
    gx[1].forward()
    gz.finish()
    gx[2].full()
    for by in (3, 1, 2):
        gy[by].forward()

    def share(by):
        gx[by].finish()
        zo = up(zh, by)
        send(s.image.at[zo, :, c], s.image.at[zo, :, c], s.gc_s.at[zo], s.gc_r.at[zo], other_core)

    share(0)
    share(3)
    share(1)
    for by in (0, 3, 1, 2):
        gy[by].finish()
    gx[2].forward()
    share(2)

    diag_shift = txt * COLS - img * (N * CHUNK)
    col_ids = lax.broadcasted_iota(jnp.int32, (STRIP, COLS), 1) + diag_shift
    row_ids = lax.broadcasted_iota(jnp.int32, (STRIP, COLS), 0)

    def diagonal(zo, first):
        return row_ids + (zo * CHUNK + first) == col_ids

    s.diag[...] = jnp.zeros((8, 128), F32)

    def chunk_stats(k, carry):
        by = jnp.where(k == 1, 3, jnp.where(k == 2, 1, jnp.where(k == 3, 2, 0)))
        zo = lax.rem(zh + by, N)
        arrive(s.image.at[zo, :, 1 - c], s.gc_s.at[zo], s.gc_r.at[zo], other_core)
        s.col_exp[zo] = LOGIT_SCALE * lax.dot_general(
            s.image[zo].reshape(CHUNK, D), s.text[...].reshape(COLS, D),
            (((1,), (1,)), ((), ())), preferred_element_type=F32,
        )
        col_peak = None
        for first in range(0, CHUNK, STRIP):
            rows = slice(first, first + STRIP)
            logits = s.col_exp[zo, rows, :]
            peak = jnp.max(logits, axis=1, keepdims=True)
            exps = jnp.exp(logits - peak)
            s.row_exp[zo, rows, :] = exps
            s.row_peak[zo, rows, :] = jnp.broadcast_to(peak, (STRIP, 128))
            log = peak + jnp.log(jnp.sum(exps, axis=1, keepdims=True))
            s.row_log[rows, :] = jnp.broadcast_to(log, (STRIP, 128))
            part = jnp.max(logits.reshape(STRIP // 8, 8, COLS), axis=0)
            col_peak = part if col_peak is None else jnp.maximum(col_peak, part)
        col_peak = jnp.max(col_peak, axis=0, keepdims=True)
        col_total = jnp.zeros((8, COLS), F32)
        diag = jnp.zeros((8, COLS), F32)
        for first in range(0, CHUNK, STRIP):
            rows = slice(first, first + STRIP)
            logits = s.col_exp[zo, rows, :]
            exps = jnp.exp(logits - col_peak)
            s.col_exp[zo, rows, :] = exps
            col_total = col_total + jnp.sum(exps.reshape(STRIP // 8, 8, COLS), axis=0)
            kept = jnp.where(diagonal(zo, first), logits, 0.0)
            diag = diag + jnp.sum(kept.reshape(STRIP // 8, 8, COLS), axis=0)
        s.diag[...] += diag[:, :128] + diag[:, 128:256] + diag[:, 256:384] + diag[:, 384:]
        s.col_peak[zo] = jnp.broadcast_to(col_peak, (8, COLS))
        col_log = col_peak + jnp.log(jnp.sum(col_total, axis=0, keepdims=True))
        s.col_log[zo] = jnp.broadcast_to(col_log, (8, COLS))
        on = eye()
        top = jnp.sum(jnp.where(on, s.row_log[0:128, :], 0.0), axis=0, keepdims=True)
        low_part = jnp.sum(jnp.where(on, s.row_log[128:256, :], 0.0), axis=0, keepdims=True)
        s.row_dense[zo] = jnp.concatenate([top, low_part] * 4, axis=0)
        return carry

    lax.fori_loop(0, N, chunk_stats, 0)

    s.row1[xc] = jnp.concatenate([s.row_dense[j][0:2] for j in range(N)], axis=0)
    exchange(s.row1, xc, N * CORES, at_xc, s.r1_s, s.r1_r)
    col_local = log_sum([s.col_log[j] for j in range(N)])[0:1]
    dense = [col_local[:, j * 128 : (j + 1) * 128] for j in range(N)]
    s.col1[y] = jnp.concatenate(dense + dense, axis=0)
    exchange(s.col1, y, N, at_y, s.c1_s, s.c1_r)
    s.row2[zh] = log_sum(collect(s.row1, xc, N * CORES, at_xc, s.r1_s, s.r1_r))
    exchange(s.row2, zh, N, at_zh, s.r2_s, s.r2_r)
    s.col2[zl] = log_sum(collect(s.col1, y, N, at_y, s.c1_s, s.c1_r))
    exchange(s.col2, zl, N, at_zl, s.c2_s, s.c2_r)
    row_lse = log_sum(collect(s.row2, zh, N, at_zh, s.r2_s, s.r2_r))
    on = eye()
    for j in range(8):
        spread = jnp.where(on, jnp.broadcast_to(row_lse[j : j + 1], (128, 128)), 0.0)
        column = jnp.sum(spread, axis=1, keepdims=True)
        rows = slice((j % 2) * 128, (j % 2) * 128 + 128)
        s.row_scale[j // 2, rows, :] = (0.5 * LOGIT_SCALE) * jnp.exp(s.row_peak[j // 2, rows, :] - column)
    col_lse = log_sum(collect(s.col2, zl, N, at_zl, s.c2_s, s.c2_r))
    wide_col = jnp.concatenate([col_lse[j : j + 1] for j in range(N)], axis=1)

    def chunk_weights(zo, carry):
        col_scale = (0.5 * LOGIT_SCALE) * jnp.exp(s.col_peak[zo, 0:1, :] - wide_col)
        for first in range(0, CHUNK, STRIP):
            rows = slice(first, first + STRIP)
            row_scale = s.row_scale[zo, rows, :]
            row_scale = jnp.concatenate([row_scale] * (COLS // 128), axis=1)
            value = s.row_exp[zo, rows, :] * row_scale + s.col_exp[zo, rows, :] * col_scale
            value = value - jnp.where(diagonal(zo, first), LOGIT_SCALE, 0.0)
            s.weights[zo, rows, :] = value.astype(BF16)
        return carry

    lax.fori_loop(0, N, chunk_weights, 0)

    share_rows = row_lse * (1.0 / (N * N * CORES))
    share_cols = col_lse * (0.5 / (N * N))
    s.loss1[xc] = share_rows + share_cols - 2.0 * s.diag[...]
    exchange(s.loss1, xc, N * CORES, at_xc, s.l1_s, s.l1_r)

    def grad_text(by):
        place = up(y, by)
        columns = pl.ds(pl.multiple_of(place * (N * ROWS), N * ROWS), N * ROWS)
        w = s.weights[:, :, columns].reshape(N * CHUNK, N * ROWS)
        out = lax.dot_general(
            w, s.image[...].reshape(N * CHUNK, D), (((0,), (0,)), ((), ())), preferred_element_type=F32
        )
        s.part_text[place] = out.astype(BF16).reshape(N, ROWS, D)

    def grad_image(by):
        zo = up(zh, by)
        out = jnp.dot(s.weights[zo], s.text[...].reshape(COLS, D), preferred_element_type=F32)
        s.part_image[zo] = out.astype(BF16).reshape(N, CORES, ROWS, D)
        send(s.part_image.at[zo, :, 1 - c], s.part_core.at[zo], s.sc_s.at[zo], s.sc_r.at[zo], other_core)

    def add_core(by):
        zo = up(zh, by)
        arrive(s.part_core.at[zo], s.sc_s.at[zo], s.sc_r.at[zo], other_core)
        s.xa[zo] = (s.part_image[zo, :, c].astype(F32) + s.part_core[zo].astype(F32)).astype(BF16)

    sx = {
        by: Scatter(
            lambda o, zo=up(zh, by): s.xa.at[zo, o],
            lambda k, zo=up(zh, by): s.xr1.at[zo, k],
            lambda k, zo=up(zh, by): s.xb.at[zo, k],
            lambda k, zo=up(zh, by): s.xr2.at[zo, k],
            x, at_x,
            lambda k, zo=up(zh, by): s.sx_s.at[zo, k],
            lambda k, zo=up(zh, by): s.sx_r.at[zo, k],
        )
        for by in range(N)
    }
    sy = {
        by: Scatter(
            lambda o, zo=up(zl, by): s.part_text.at[o, zo],
            lambda k, zo=up(zl, by): s.yr1.at[zo, k],
            lambda k, zo=up(zl, by): s.yb.at[zo, k],
            lambda k, zo=up(zl, by): s.yr2.at[zo, k],
            y, at_y,
            lambda k, zo=up(zl, by): s.sy_s.at[zo, k],
            lambda k, zo=up(zl, by): s.sy_r.at[zo, k],
        )
        for by in range(N)
    }
    sz = Scatter(
        lambda o: s.za.at[o], lambda k: s.zr1.at[k], lambda k: s.zb.at[k], lambda k: s.zr2.at[k],
        zh, at_zh, lambda k: s.sz_s.at[k], lambda k: s.sz_r.at[k],
    )

    grad_text(2)
    for by in (2, 1, 3, 0):
        sy[by].first()
    grad_image(2)
    grad_text(1)
    grad_text(3)
    add_core(2)
    sx[2].first()
    grad_image(1)
    for by in (2, 1, 3, 0):
        sy[by].second()
    add_core(1)
    sx[1].first()
    grad_image(3)
    sx[2].second()
    add_core(3)
    sx[3].first()
    grad_image(0)
    grad_text(0)
    sx[1].second()
    add_core(0)
    sx[0].first()
    sx[3].second()

    s.za[up(zh, 2)] = sx[2].third()
    sz.first()
    for by in (2, 1, 3):
        peer = up(zl, by)
        s.ta[peer] = sy[by].third()
        send(s.ta.at[peer], s.tr.at[zl], s.sl_s.at[by], s.sl_r.at[by], at_zl(peer))
    sx[0].second()
    s.za[up(zh, 1)] = sx[1].third()
    s.za[up(zh, 3)] = sx[3].third()
    sz.second()

    s.loss2[zh] = sum(collect(s.loss1, xc, N * CORES, at_xc, s.l1_s, s.l1_r))
    exchange(s.loss2, zh, N, at_zh, s.l2_s, s.l2_r)
    text_total = sy[0].third().astype(F32)
    s.loss3[y] = sum(collect(s.loss2, zh, N, at_zh, s.l2_s, s.l2_r))
    exchange(s.loss3, y, N, at_y, s.l3_s, s.l3_r)
    s.za[zh] = sx[0].third()
    s.loss4[zl] = sum(collect(s.loss3, y, N, at_y, s.l3_s, s.l3_r))
    exchange(s.loss4, zl, N, at_zl, s.l4_s, s.l4_r)
    for by in (1, 3, 2):
        peer = up(zl, N - by)
        arrive(s.tr.at[peer], s.sl_s.at[by], s.sl_r.at[by], at_zl(peer))
        text_total = text_total + s.tr[peer].astype(F32)
    gt_out[0] = text_total.astype(BF16)
    gi_out[...] = sz.third()
    total = sum(collect(s.loss4, zl, N, at_zl, s.l4_s, s.l4_r))
    loss_out[0, 0] = jnp.sum(total) / (2.0 * PAIRS)

    for copy in sent:
        copy.wait_send()


def per_device(images, texts):
    loss, grad_images, grad_texts = pl.pallas_call(
        kernel,
        out_shape=(
            jax.ShapeDtypeStruct((1, 1), F32),
            jax.ShapeDtypeStruct((ROWS, D), BF16),
            jax.ShapeDtypeStruct((1, ROWS, D), BF16),
        ),
        in_specs=[pl.BlockSpec(memory_space=pl.ANY)] * 2,
        out_specs=(
            pl.BlockSpec(memory_space=pltpu.SMEM),
            pl.BlockSpec(memory_space=pltpu.VMEM),
            pl.BlockSpec(memory_space=pltpu.VMEM),
        ),
        scratch_shapes=list(SCRATCH.values()),
        compiler_params=pltpu.CompilerParams(
            collective_id=0, has_side_effects=True, vmem_limit_bytes=48 * 1024 * 1024
        ),
        name="contrastive",
    )(images, texts)
    return loss.reshape(()), grad_images, grad_texts


def solution(mesh):
    in_specs = (P(("img", "txt"), None), P("img", "txt", None))
    out_specs = (P(), P(("img", "txt"), None), P("img", "txt", None))
    return jax.shard_map(
        per_device, mesh=mesh, in_specs=in_specs, out_specs=out_specs, check_vma=False
    )
```

```python
import jax
import jax.numpy as jnp
from jax import lax
from jax.experimental import pallas as pl
from jax.experimental.pallas import tpu as pltpu
from jax.sharding import PartitionSpec as P

LOGIT_SCALE = 1.0 / 0.07
MESH = pl.DeviceIdType.MESH
F32 = jnp.float32
BF16 = jnp.bfloat16

N = 4
NZ = 16
CORES = 2
ROWS = 32
D = 1024
WIDE = D // 2
CHUNK = N * ROWS
COLS = N * N * CORES * ROWS
PAIRS = 16384
STRIP = ROWS
FAR = NZ // 2

PIECES = [(pl.ds(0, 16), pl.ds(0, D)), (pl.ds(16, 16), pl.ds(0, D))]
NP = len(PIECES)
UPPER = list(range(NP // 2))
LOWER = list(range(NP // 2, NP))


def dma(*shape):
    return pltpu.SemaphoreType.DMA(shape)


def bf16(*shape):
    return pltpu.VMEM(shape, BF16)


def f32(*shape):
    return pltpu.VMEM(shape, F32)


SCRATCH = dict(
    image=bf16(NZ, ROWS, D),
    text=bf16(N, N, CORES, ROWS, D),
    row_exp=f32(N, CHUNK, COLS),
    col_exp=f32(N, CHUNK, COLS),
    row_peak=f32(N, CHUNK, 128),
    row_scale=f32(N, CHUNK, 128),
    row_log=f32(CHUNK, 128),
    row_dense=f32(N, 8, 128),
    col_peak=f32(N, 8, COLS),
    col_log=f32(N, 8, COLS),
    col_ids=pltpu.VMEM((8, COLS), jnp.int32),
    diag=f32(8, 128),
    weights=bf16(N, CHUNK, COLS),
    part_image=bf16(NZ, ROWS, D),
    z_in=bf16(2, FAR + 1, ROWS, D),
    z_out=bf16(2, FAR + 1, ROWS, D),
    part_text=bf16(N, N, CORES, ROWS, D),
    part_core=bf16(N, N, ROWS, D),
    plane=bf16(N, N, ROWS, D),
    big_in=bf16(2, N, 3, ROWS, WIDE),
    big_out=bf16(2, N, ROWS, WIDE),
    line=bf16(2, N, ROWS, WIDE),
    small_in=bf16(2, 3, ROWS, WIDE),
    small_out=bf16(2, ROWS, WIDE),
    row1=f32(NZ, N, 128),
    col1=f32(N * CORES, 8, 128),
    col2=f32(N, 8, 128),
    loss1=f32(N * CORES, 1, 128),
    loss2=f32(N, 1, 128),
    loss3=f32(NZ, 1, 128),
    local_sem=dma(2),
    zg_s=dma(2, FAR + 1, NP), zg_r=dma(2, FAR + 1, NP),
    small_g_s=dma(2, 3), small_g_r=dma(2, 3),
    big_g_s=dma(2, N, 3), big_g_r=dma(2, N, 3),
    core_g_s=dma(2, N), core_g_r=dma(2, N),
    row1_s=dma(NZ), row1_r=dma(NZ),
    col1_s=dma(N * CORES), col1_r=dma(N * CORES),
    col2_s=dma(N), col2_r=dma(N),
    loss1_s=dma(N * CORES), loss1_r=dma(N * CORES),
    loss2_s=dma(N), loss2_r=dma(N),
    loss3_s=dma(NZ), loss3_r=dma(NZ),
    core_s_s=dma(N), core_s_r=dma(N),
    zs_s=dma(2, FAR + 1, NP), zs_r=dma(2, FAR + 1, NP),
    big_s_s=dma(2, N, 3), big_s_r=dma(2, N, 3),
    small_s_s=dma(2, 3), small_s_r=dma(2, 3),
)
NAMES = list(SCRATCH)


class Refs:
    def __init__(self, refs):
        for name, ref in zip(NAMES, refs):
            setattr(self, name, ref)


def log_sum(parts):
    peak = parts[0]
    for part in parts[1:]:
        peak = jnp.maximum(peak, part)
    total = jnp.exp(parts[0] - peak)
    for part in parts[1:]:
        total = total + jnp.exp(part - peak)
    return peak + jnp.log(total)


def eye():
    rows = lax.broadcasted_iota(jnp.int32, (128, 128), 0)
    cols = lax.broadcasted_iota(jnp.int32, (128, 128), 1)
    return rows == cols


def add(a, b):
    return (a.astype(F32) + b.astype(F32)).astype(BF16)


def kernel(img_hbm, txt_hbm, loss_out, gi_out, gt_out, *refs):
    s = Refs(refs)
    img, txt = lax.axis_index("img"), lax.axis_index("txt")
    y, zl = img // N, lax.rem(img, N)
    zh, xc = txt // (N * CORES), lax.rem(txt, N * CORES)
    x, c = xc // CORES, lax.rem(xc, CORES)
    z = zh * N + zl

    def up(place, by, count=N):
        return lax.rem(place + (by + count) % count, count)

    def at_x(place):
        return (img, (zh * N + place) * CORES + c)

    def at_xc(place):
        return (img, zh * (N * CORES) + place)

    def at_y(place):
        return (place * N + zl, txt)

    def at_z(place):
        return (y * N + lax.rem(place, N), (place // N) * (N * CORES) + xc)

    other_core = (img, (zh * N + x) * CORES + (1 - c))

    own_image = pltpu.make_async_copy(img_hbm, s.image.at[z], s.local_sem.at[0])
    own_text = pltpu.make_async_copy(txt_hbm.at[0], s.text.at[y, x, c], s.local_sem.at[1])
    own_image.start()
    own_text.start()

    barrier = pltpu.get_barrier_semaphore()
    z_right, z_left = at_z(up(z, 1, NZ)), at_z(up(z, -1, NZ))
    partners = [z_right, z_left]
    partners += [at_y(up(y, by)) for by in range(1, N)]
    partners += [at_xc(up(xc, by, N * CORES)) for by in range(1, N * CORES)]
    for partner in partners:
        pl.semaphore_signal(barrier, inc=1, device_id=partner, device_id_type=MESH)
    lane = lax.broadcasted_iota(jnp.int32, (8, COLS), 1)
    s.col_ids[...] = (
        zh * 4096 + lax.rem(lane // 64, 4) * 1024 + lax.rem(lane // 32, 2) * 512
        + (lane // 256) * 128 + zl * 32 + lax.rem(lane, 32)
    )
    pl.semaphore_wait(barrier, len(partners))

    sent = []

    def remote(src, dst, send_sem, recv_sem, device):
        return pltpu.make_async_remote_copy(
            src_ref=src, dst_ref=dst, send_sem=send_sem, recv_sem=recv_sem,
            device_id=device, device_id_type=MESH,
        )

    def send(*args):
        copy = remote(*args)
        copy.start()
        sent.append(copy)

    def arrive(dst, send_sem, recv_sem, device):
        remote(dst, dst, send_sem, recv_sem, device).wait_recv()

    def exchange(buf, me, count, device, ss, rs):
        for by in sorted(range(1, count), key=lambda k: -min(k, count - k)):
            peer = up(me, by, count)
            send(buf.at[me], buf.at[me], ss.at[by], rs.at[by], device(peer))

    def collect(buf, me, count, device, ss, rs):
        for by in sorted(range(1, count), key=lambda k: min(k, count - k)):
            peer = up(me, -by, count)
            arrive(buf.at[peer], ss.at[by], rs.at[by], device(peer))
        return [buf[j] for j in range(count)]

    class Gather:
        def __init__(self, slot, me, device, ss, rs, far_right):
            self.slot, self.me, self.device, self.ss, self.rs = slot, me, device, ss, rs
            self.right, self.left, self.far = up(me, 1), up(me, -1), up(me, 2)
            self.far_right = far_right

        def full(self):
            own = self.slot(self.me)
            pair = [(0, self.right), (1, self.left)]
            for k, to in pair if self.far_right else pair[::-1]:
                send(own, own, self.ss.at[k], self.rs.at[k], self.device(to))

        def forward(self):
            pair = [(0, self.left, self.right), (1, self.right, self.left)]
            for k, origin, to in pair if self.far_right else pair[::-1]:
                block = self.slot(origin)
                arrive(block, self.ss.at[k], self.rs.at[k], self.device(origin))
                if (k == 0) == self.far_right:
                    send(block, block, self.ss.at[2], self.rs.at[2], self.device(to))

        def finish(self):
            origin = self.left if self.far_right else self.right
            arrive(self.slot(self.far), self.ss.at[2], self.rs.at[2], self.device(origin))

    class Scatter:
        def __init__(self, slot, r, b, me, device, ss, rs, far_right):
            self.slot, self.r, self.b = slot, r, b
            self.me, self.device, self.ss, self.rs = me, device, ss, rs
            self.far = up(me, 2)
            self.ahead, self.behind = (up(me, 1), up(me, -1)) if far_right else (up(me, -1), up(me, 1))

        def first(self):
            send(self.slot(self.far), self.r.at[0], self.ss.at[0], self.rs.at[0], self.device(self.ahead))
            send(self.slot(self.behind), self.r.at[1], self.ss.at[1], self.rs.at[1], self.device(self.behind))

        def second(self):
            arrive(self.r.at[0], self.ss.at[0], self.rs.at[0], self.device(self.behind))
            self.b[...] = add(self.slot(self.ahead)[...], self.r[0])
            send(self.b, self.r.at[2], self.ss.at[2], self.rs.at[2], self.device(self.ahead))

        def third(self):
            arrive(self.r.at[1], self.ss.at[1], self.rs.at[1], self.device(self.ahead))
            arrive(self.r.at[2], self.ss.at[2], self.rs.at[2], self.device(self.behind))
            total = self.slot(self.me)[...].astype(F32) + self.r[1].astype(F32)
            return (total + self.r[2].astype(F32)).astype(BF16)

    halves = [pl.ds(0, WIDE), pl.ds(WIDE, WIDE)]
    small_g = [
        Gather(lambda o: s.text.at[y, o, c, :, halves[0]], x, at_x, s.small_g_s.at[0], s.small_g_r.at[0], True),
        Gather(lambda o: s.text.at[o, x, c, :, halves[1]], y, at_y, s.small_g_s.at[1], s.small_g_r.at[1], True),
    ]
    big_g = [
        {
            by: Gather(
                lambda o, q=up(x, by): s.text.at[o, q, c, :, halves[0]], y, at_y,
                s.big_g_s.at[0, up(x, by)], s.big_g_r.at[0, up(x, by)], by % 2 == 0,
            )
            for by in range(N)
        },
        {
            by: Gather(
                lambda o, q=up(y, by): s.text.at[q, o, c, :, halves[1]], x, at_x,
                s.big_g_s.at[1, up(y, by)], s.big_g_r.at[1, up(y, by)], by % 2 == 0,
            )
            for by in range(N)
        },
    ]

    def core_block(h, by, core):
        if h == 0:
            return s.text.at[:, up(x, by), core, :, halves[0]]
        return s.text.at[up(y, by), :, core, :, halves[1]]

    def share(by):
        for h in range(2):
            big_g[h][by].finish()
            q = up(x, by) if h == 0 else up(y, by)
            block = core_block(h, by, c)
            send(block, block, s.core_g_s.at[h, q], s.core_g_r.at[h, q], other_core)

    def z_piece(ref, p):
        return ref.at[PIECES[p][0], PIECES[p][1]]

    def z_own():
        for p in range(NP):
            block = z_piece(s.image.at[z], p)
            send(block, block, s.zg_s.at[0, 1, p], s.zg_r.at[0, 1, p], z_right)
            send(block, block, s.zg_s.at[1, 1, p], s.zg_r.at[1, 1, p], z_left)

    def z_gather(step):
        for p in range(NP):
            for way in range(2):
                if step == FAR and p not in (UPPER, LOWER)[way]:
                    continue
                origin = up(z, -step if way == 0 else step, NZ)
                source, target = (z_left, z_right) if way == 0 else (z_right, z_left)
                block = z_piece(s.image.at[origin], p)
                arrive(block, s.zg_s.at[way, step, p], s.zg_r.at[way, step, p], source)
                if step < FAR - 1 or (step == FAR - 1 and p in (UPPER, LOWER)[way]):
                    send(block, block, s.zg_s.at[way, step + 1, p], s.zg_r.at[way, step + 1, p], target)

    own_image.wait()
    z_own()
    own_text.wait()
    for h in range(2):
        small_g[h].full()
    for h in range(2):
        big_g[h][0].full()
    z_gather(1)
    for h in range(2):
        small_g[h].forward()
        big_g[h][3].full()
        big_g[h][1].full()
    z_gather(2)
    for h in range(2):
        small_g[h].finish()
        big_g[h][2].full()
        big_g[h][0].forward()
    z_gather(3)
    for by in (3, 1):
        for h in range(2):
            big_g[h][by].forward()
    share(0)
    z_gather(4)
    for h in range(2):
        big_g[h][2].forward()
    share(3)
    share(1)
    z_gather(5)
    share(2)
    z_gather(6)
    for by in (0, 3, 1, 2):
        for h in range(2):
            q = up(x, by) if h == 0 else up(y, by)
            arrive(core_block(h, by, 1 - c), s.core_g_s.at[h, q], s.core_g_r.at[h, q], other_core)
    z_gather(7)

    row_place = lax.broadcasted_iota(jnp.int32, (STRIP, COLS), 0)

    def diagonal(q, strip):
        first = y * 4096 + strip * 1024 + (q * N + x) * 64 + c * 32
        return row_place + first == s.col_ids[0:1, :]

    s.diag[...] = jnp.zeros((8, 128), F32)

    def chunk_stats(by):
        q = lax.rem(zh + by, N)
        images = s.image[pl.ds(q * N, N)].reshape(CHUNK, D)
        s.col_exp[q] = LOGIT_SCALE * lax.dot_general(
            images, s.text[...].reshape(COLS, D), (((1,), (1,)), ((), ())), preferred_element_type=F32
        )
        col_peak = None
        for strip in range(N):
            rows = slice(strip * STRIP, (strip + 1) * STRIP)
            logits = s.col_exp[q, rows, :]
            peak = jnp.max(logits, axis=1, keepdims=True)
            exps = jnp.exp(logits - peak)
            s.row_exp[q, rows, :] = exps
            s.row_peak[q, rows, :] = jnp.broadcast_to(peak, (STRIP, 128))
            log = peak + jnp.log(jnp.sum(exps, axis=1, keepdims=True))
            s.row_log[rows, :] = jnp.broadcast_to(log, (STRIP, 128))
            part = jnp.max(logits.reshape(STRIP // 8, 8, COLS), axis=0)
            col_peak = part if col_peak is None else jnp.maximum(col_peak, part)
        col_peak = jnp.max(col_peak, axis=0, keepdims=True)
        col_total = jnp.zeros((8, COLS), F32)
        diag = jnp.zeros((8, COLS), F32)
        for strip in range(N):
            rows = slice(strip * STRIP, (strip + 1) * STRIP)
            logits = s.col_exp[q, rows, :]
            exps = jnp.exp(logits - col_peak)
            s.col_exp[q, rows, :] = exps
            col_total = col_total + jnp.sum(exps.reshape(STRIP // 8, 8, COLS), axis=0)
            kept = jnp.where(diagonal(q, strip), logits, 0.0)
            diag = diag + jnp.sum(kept.reshape(STRIP // 8, 8, COLS), axis=0)
        s.diag[...] += sum(diag[:, j * 128 : (j + 1) * 128] for j in range(COLS // 128))
        s.col_peak[q] = jnp.broadcast_to(col_peak, (8, COLS))
        col_log = col_peak + jnp.log(jnp.sum(col_total, axis=0, keepdims=True))
        s.col_log[q] = jnp.broadcast_to(col_log, (8, COLS))
        dense = jnp.sum(jnp.where(eye(), s.row_log[...], 0.0), axis=0, keepdims=True)
        s.row_dense[q] = jnp.broadcast_to(dense, (8, 128))

    def near_chunk(k, carry):
        chunk_stats(jnp.where(k == 2, 3, k))
        return carry

    lax.fori_loop(0, 3, near_chunk, 0)
    z_gather(8)
    chunk_stats(2)

    s.row1[z] = jnp.concatenate([s.row_dense[j][0:1] for j in range(N)], axis=0)
    exchange(s.row1, z, NZ, at_z, s.row1_s, s.row1_r)
    col_local = log_sum([s.col_log[j] for j in range(N)])[0:1]
    s.col1[xc] = jnp.concatenate([col_local[:, j * 128 : (j + 1) * 128] for j in range(8)], axis=0)
    exchange(s.col1, xc, N * CORES, at_xc, s.col1_s, s.col1_r)
    s.col2[y] = log_sum(collect(s.col1, xc, N * CORES, at_xc, s.col1_s, s.col1_r))
    exchange(s.col2, y, N, at_y, s.col2_s, s.col2_r)
    col_lse = log_sum(collect(s.col2, y, N, at_y, s.col2_s, s.col2_r))
    wide_col = jnp.concatenate([col_lse[j : j + 1] for j in range(8)], axis=1)
    row_lse = log_sum(collect(s.row1, z, NZ, at_z, s.row1_s, s.row1_r))
    on = eye()
    for j in range(N):
        spread = jnp.where(on, jnp.broadcast_to(row_lse[j : j + 1], (128, 128)), 0.0)
        column = jnp.sum(spread, axis=1, keepdims=True)
        s.row_scale[j] = (0.5 * LOGIT_SCALE) * jnp.exp(s.row_peak[j] - column)

    def chunk_weights(q, carry):
        col_scale = (0.5 * LOGIT_SCALE) * jnp.exp(s.col_peak[q, 0:1, :] - wide_col)
        for strip in range(N):
            rows = slice(strip * STRIP, (strip + 1) * STRIP)
            row_scale = jnp.concatenate([s.row_scale[q, rows, :]] * (COLS // 128), axis=1)
            value = s.row_exp[q, rows, :] * row_scale + s.col_exp[q, rows, :] * col_scale
            value = value - jnp.where(diagonal(q, strip), LOGIT_SCALE, 0.0)
            s.weights[q, rows, :] = value.astype(BF16)
        return carry

    lax.fori_loop(0, N, chunk_weights, 0)

    def grad_image(by):
        q = up(zh, by)
        out = jnp.dot(s.weights[q], s.text[...].reshape(COLS, D), preferred_element_type=F32)
        s.part_image[pl.ds(q * N, N)] = out.astype(BF16).reshape(N, ROWS, D)

    def z_scatter(step):
        for p in range(NP):
            for way in range(2):
                mine = p in (UPPER, LOWER)[way]
                if step == 1 and not mine:
                    continue
                by = FAR + 1 - step
                block = z_piece(s.part_image.at[up(z, by if way == 0 else -by, NZ)], p)
                source, target = (z_left, z_right) if way == 0 else (z_right, z_left)
                if step > 2 or (step == 2 and mine):
                    got = z_piece(s.z_in.at[way, step - 1], p)
                    arrive(got, s.zs_s.at[way, step - 1, p], s.zs_r.at[way, step - 1, p], source)
                    out = z_piece(s.z_out.at[way, step], p)
                    out[...] = add(block[...], got[...])
                    block = out
                there = z_piece(s.z_in.at[way, step], p)
                send(block, there, s.zs_s.at[way, step, p], s.zs_r.at[way, step, p], target)

    def z_last():
        for p in range(NP):
            total = z_piece(s.part_image.at[z], p)[...].astype(F32)
            for way in range(2):
                got = z_piece(s.z_in.at[way, FAR], p)
                source = (z_left, z_right)[way]
                arrive(got, s.zs_s.at[way, FAR, p], s.zs_r.at[way, FAR, p], source)
                total = total + got[...].astype(F32)
            gi_out[PIECES[p][0], PIECES[p][1]] = total.astype(BF16)

    def grad_text(by):
        place = up(y, by)
        wide = N * CORES * ROWS
        columns = pl.ds(pl.multiple_of(place * wide, wide), wide)
        w = s.weights[:, :, columns].reshape(N * CHUNK, wide)
        out = lax.dot_general(
            w, s.image[...].reshape(NZ * ROWS, D), (((0,), (0,)), ((), ())), preferred_element_type=F32
        )
        s.part_text[place] = out.astype(BF16).reshape(N, CORES, ROWS, D)
        send(s.part_text.at[place, :, 1 - c], s.part_core.at[place], s.core_s_s.at[by], s.core_s_r.at[by], other_core)

    def add_core(by):
        place = up(y, by)
        arrive(s.part_core.at[place], s.core_s_s.at[by], s.core_s_r.at[by], other_core)
        s.plane[place] = add(s.part_text[place, :, c], s.part_core[place])

    big_s = [
        {
            by: Scatter(
                lambda o, q=up(x, by): s.plane.at[o, q, :, halves[0]],
                s.big_in.at[0, up(x, by)], s.big_out.at[0, up(x, by)], y, at_y,
                s.big_s_s.at[0, up(x, by)], s.big_s_r.at[0, up(x, by)], by % 2 == 0,
            )
            for by in range(N)
        },
        {
            by: Scatter(
                lambda o, q=up(y, by): s.plane.at[q, o, :, halves[1]],
                s.big_in.at[1, up(y, by)], s.big_out.at[1, up(y, by)], x, at_x,
                s.big_s_s.at[1, up(y, by)], s.big_s_r.at[1, up(y, by)], by % 2 == 0,
            )
            for by in range(N)
        },
    ]
    small_s = [
        Scatter(
            lambda o: s.line.at[0, o], s.small_in.at[0], s.small_out.at[0], x, at_x,
            s.small_s_s.at[0], s.small_s_r.at[0], True,
        ),
        Scatter(
            lambda o: s.line.at[1, o], s.small_in.at[1], s.small_out.at[1], y, at_y,
            s.small_s_s.at[1], s.small_s_r.at[1], True,
        ),
    ]

    def fold(by):
        for h in range(2):
            q = up(x, by) if h == 0 else up(y, by)
            s.line[h, q] = big_s[h][by].third()

    grad_image(2)
    z_scatter(1)
    grad_image(1)
    grad_image(3)
    z_scatter(2)
    grad_image(0)
    for by in (2, 1, 3, 0):
        grad_text(by)
    z_scatter(3)

    share_rows = jnp.sum(row_lse) * (1.0 / NZ)
    share_cols = jnp.sum(col_lse) * (1.0 / (N * N * CORES))
    own_share = share_rows + share_cols - 2.0 * jnp.sum(s.diag[...])
    s.loss1[xc] = jnp.full((1, 128), own_share, F32)
    exchange(s.loss1, xc, N * CORES, at_xc, s.loss1_s, s.loss1_r)

    for by in (2, 1, 3, 0):
        add_core(by)
        big_s[1][by].first()
    for by in (2, 1, 3, 0):
        big_s[0][by].first()
    z_scatter(4)
    for by in (2, 1):
        big_s[1][by].second()
    z_scatter(5)
    for by in (3, 0):
        big_s[1][by].second()
    s.loss2[y] = sum(collect(s.loss1, xc, N * CORES, at_xc, s.loss1_s, s.loss1_r))
    exchange(s.loss2, y, N, at_y, s.loss2_s, s.loss2_r)
    for by in (2, 1, 3, 0):
        big_s[0][by].second()
    z_scatter(6)
    fold(2)
    fold(1)
    fold(3)
    s.loss3[z] = sum(collect(s.loss2, y, N, at_y, s.loss2_s, s.loss2_r))
    exchange(s.loss3, z, NZ, at_z, s.loss3_s, s.loss3_r)
    z_scatter(7)
    for h in range(2):
        small_s[h].first()
    fold(0)
    z_scatter(8)
    for h in range(2):
        small_s[h].second()
    for h in range(2):
        gt_out[0, :, halves[h]] = small_s[h].third()
    total = sum(collect(s.loss3, z, NZ, at_z, s.loss3_s, s.loss3_r))
    loss_out[0, 0] = jnp.max(total) / (2.0 * PAIRS)
    z_last()

    for copy in sent:
        copy.wait_send()


def per_device(images, texts):
    loss, grad_images, grad_texts = pl.pallas_call(
        kernel,
        out_shape=(
            jax.ShapeDtypeStruct((1, 1), F32),
            jax.ShapeDtypeStruct((ROWS, D), BF16),
            jax.ShapeDtypeStruct((1, ROWS, D), BF16),
        ),
        in_specs=[pl.BlockSpec(memory_space=pl.ANY)] * 2,
        out_specs=(
            pl.BlockSpec(memory_space=pltpu.SMEM),
            pl.BlockSpec(memory_space=pltpu.VMEM),
            pl.BlockSpec(memory_space=pltpu.VMEM),
        ),
        scratch_shapes=list(SCRATCH.values()),
        compiler_params=pltpu.CompilerParams(
            collective_id=0, has_side_effects=True, vmem_limit_bytes=48 * 1024 * 1024
        ),
        name="contrastive",
    )(images, texts)
    return loss.reshape(()), grad_images, grad_texts


def solution(mesh):
    in_specs = (P(("img", "txt"), None), P("img", "txt", None))
    out_specs = (P(), P(("img", "txt"), None), P("img", "txt", None))
    return jax.shard_map(
        per_device, mesh=mesh, in_specs=in_specs, out_specs=out_specs, check_vma=False
    )
```

```python
import jax
import jax.numpy as jnp
from jax import lax
from jax.experimental import pallas as pl
from jax.experimental.pallas import tpu as pltpu
from jax.sharding import PartitionSpec as P

LOGIT_SCALE = 1.0 / 0.07
MESH = pl.DeviceIdType.MESH
F32 = jnp.float32
BF16 = jnp.bfloat16

N = 4
NZ = 16
CORES = 2
ROWS = 32
D = 1024
WIDE = D // 2
CHUNK = N * ROWS
COLS = N * N * CORES * ROWS
PAIRS = 16384
STRIP = ROWS
FAR = NZ // 2

def dma(*shape):
    return pltpu.SemaphoreType.DMA(shape)


def bf16(*shape):
    return pltpu.VMEM(shape, BF16)


def f32(*shape):
    return pltpu.VMEM(shape, F32)


SCRATCH = dict(
    image=bf16(NZ, ROWS, D),
    text=bf16(N, N, CORES, ROWS, D),
    row_exp=f32(N, CHUNK, COLS),
    col_exp=f32(N, CHUNK, COLS),
    row_peak=f32(N, CHUNK, 128),
    row_scale=f32(N, CHUNK, 128),
    row_log=f32(CHUNK, 128),
    row_dense=f32(N, 8, 128),
    col_peak=f32(N, 8, COLS),
    col_log=f32(N, 8, COLS),
    col_ids=pltpu.VMEM((8, COLS), jnp.int32),
    diag=f32(8, 128),
    weights=bf16(N, CHUNK, COLS),
    part_image=bf16(NZ, ROWS, D),
    z_in=bf16(2, FAR + 1, ROWS, D),
    z_out=bf16(2, 2, ROWS, D),
    part_text=bf16(N, N, CORES, ROWS, D),
    part_core=bf16(N, N, ROWS, D),
    plane=bf16(N, N, ROWS, D),
    big_in=bf16(2, N, N, ROWS, WIDE),
    line=bf16(2, N, ROWS, WIDE),
    small_in=bf16(2, N, ROWS, WIDE),
    row1=f32(NZ, N, 128),
    col1=f32(N * CORES, 8, 128),
    col2=f32(N, 8, 128),
    loss1=f32(N * CORES, 1, 128),
    loss2=f32(N, 1, 128),
    loss3=f32(NZ, 1, 128),
    local_sem=dma(2),
    zg_s=dma(2, FAR + 1), zg_r=dma(2, FAR + 1),
    small_g_s=dma(2, N), small_g_r=dma(2, N),
    big_g_s=dma(2, N, N), big_g_r=dma(2, N, N),
    core_g_s=dma(2, N), core_g_r=dma(2, N),
    row1_s=dma(NZ), row1_r=dma(NZ),
    col1_s=dma(N * CORES), col1_r=dma(N * CORES),
    col2_s=dma(N), col2_r=dma(N),
    loss1_s=dma(N * CORES), loss1_r=dma(N * CORES),
    loss2_s=dma(N), loss2_r=dma(N),
    loss3_s=dma(NZ), loss3_r=dma(NZ),
    core_s_s=dma(N), core_s_r=dma(N),
    zs_s=dma(2, FAR + 1), zs_r=dma(2, FAR + 1),
    big_s_s=dma(2, N, N), big_s_r=dma(2, N, N),
    small_s_s=dma(2, N), small_s_r=dma(2, N),
)
NAMES = list(SCRATCH)


class Refs:
    def __init__(self, refs):
        for name, ref in zip(NAMES, refs):
            setattr(self, name, ref)


def log_sum(parts):
    peak = parts[0]
    for part in parts[1:]:
        peak = jnp.maximum(peak, part)
    total = jnp.exp(parts[0] - peak)
    for part in parts[1:]:
        total = total + jnp.exp(part - peak)
    return peak + jnp.log(total)


def eye():
    rows = lax.broadcasted_iota(jnp.int32, (128, 128), 0)
    cols = lax.broadcasted_iota(jnp.int32, (128, 128), 1)
    return rows == cols


def add(a, b):
    return (a.astype(F32) + b.astype(F32)).astype(BF16)


def kernel(img_hbm, txt_hbm, loss_out, gi_out, gt_out, *refs):
    s = Refs(refs)
    img, txt = lax.axis_index("img"), lax.axis_index("txt")
    y, zl = img // N, lax.rem(img, N)
    zh, xc = txt // (N * CORES), lax.rem(txt, N * CORES)
    x, c = xc // CORES, lax.rem(xc, CORES)
    z = zh * N + zl

    def up(place, by, count=N):
        return lax.rem(place + (by + count) % count, count)

    def at_x(place):
        return (img, (zh * N + place) * CORES + c)

    def at_xc(place):
        return (img, zh * (N * CORES) + place)

    def at_y(place):
        return (place * N + zl, txt)

    def at_z(place):
        return (y * N + lax.rem(place, N), (place // N) * (N * CORES) + xc)

    other_core = (img, (zh * N + x) * CORES + (1 - c))

    own_image = pltpu.make_async_copy(img_hbm, s.image.at[z], s.local_sem.at[0])
    own_text = pltpu.make_async_copy(txt_hbm.at[0], s.text.at[y, x, c], s.local_sem.at[1])
    own_image.start()
    own_text.start()

    barrier = pltpu.get_barrier_semaphore()
    partners = [at_z(up(z, by, NZ)) for by in (3, -3, 2, -2, 1, -1)]
    partners += [at_y(up(y, by)) for by in range(1, N)] + [at_x(up(x, by)) for by in range(1, N)]
    partners += [other_core]
    for partner in partners:
        pl.semaphore_signal(barrier, inc=1, device_id=partner, device_id_type=MESH)
    lane = lax.broadcasted_iota(jnp.int32, (8, COLS), 1)
    s.col_ids[...] = (
        zh * 4096 + lax.rem(lane // 64, 4) * 1024 + lax.rem(lane // 32, 2) * 512
        + (lane // 256) * 128 + zl * 32 + lax.rem(lane, 32)
    )
    pl.semaphore_wait(barrier, len(partners))

    sent = []

    def remote(src, dst, send_sem, recv_sem, device):
        return pltpu.make_async_remote_copy(
            src_ref=src, dst_ref=dst, send_sem=send_sem, recv_sem=recv_sem,
            device_id=device, device_id_type=MESH,
        )

    def send(*args):
        copy = remote(*args)
        copy.start()
        sent.append(copy)

    def arrive(dst, send_sem, recv_sem, device):
        remote(dst, dst, send_sem, recv_sem, device).wait_recv()

    def exchange(buf, me, count, device, ss, rs):
        for by in sorted(range(1, count), key=lambda k: -min(k, count - k)):
            peer = up(me, by, count)
            send(buf.at[me], buf.at[me], ss.at[by], rs.at[by], device(peer))

    def collect(buf, me, count, device, ss, rs):
        for by in sorted(range(1, count), key=lambda k: min(k, count - k)):
            peer = up(me, -by, count)
            arrive(buf.at[peer], ss.at[by], rs.at[by], device(peer))
        return [buf[j] for j in range(count)]

    class Gather:
        def __init__(self, slot, me, device, ss, rs):
            self.slot, self.me, self.device, self.ss, self.rs = slot, me, device, ss, rs

        def start(self):
            own = self.slot(self.me)
            for by in (2, 1, 3):
                send(own, own, self.ss.at[by], self.rs.at[by], self.device(up(self.me, by)))

        def wait(self, by):
            origin = up(self.me, by)
            arrive(self.slot(origin), self.ss.at[N - by], self.rs.at[N - by], self.device(origin))

    class Scatter:
        def __init__(self, slot, r, me, device, ss, rs):
            self.slot, self.r = slot, r
            self.me, self.device, self.ss, self.rs = me, device, ss, rs

        def start(self):
            for by in (2, 1, 3):
                to = up(self.me, by)
                send(self.slot(to), self.r.at[by], self.ss.at[by], self.rs.at[by], self.device(to))

        def finish(self):
            total = self.slot(self.me)[...].astype(F32)
            for by in (1, 3, 2):
                arrive(self.r.at[by], self.ss.at[by], self.rs.at[by], self.device(up(self.me, -by)))
                total = total + self.r[by].astype(F32)
            return total.astype(BF16)

    upper, lower = pl.ds(0, ROWS // 2), pl.ds(ROWS // 2, ROWS // 2)
    ends = (upper, lower)

    def along(way, steps):
        return at_z(up(z, steps if way == 0 else -steps, NZ))

    def z_block(way, steps):
        block = s.image.at[up(z, -steps if way == 0 else steps, NZ)]
        return block.at[ends[way]] if steps == FAR else block

    def z_send(way, held, reach):
        block = s.image.at[up(z, -held if way == 0 else held, NZ)]
        if reach == FAR:
            block = block.at[ends[way]]
        send(block, block, s.zg_s.at[way, reach], s.zg_r.at[way, reach], along(way, reach - held))

    def z_wait(way, steps):
        arrive(z_block(way, steps), s.zg_s.at[way, steps], s.zg_r.at[way, steps], along(way, -1))

    halves = [pl.ds(0, WIDE), pl.ds(WIDE, WIDE)]
    small_g = [
        Gather(lambda o: s.text.at[y, o, c, :, halves[0]], x, at_x, s.small_g_s.at[0], s.small_g_r.at[0]),
        Gather(lambda o: s.text.at[o, x, c, :, halves[1]], y, at_y, s.small_g_s.at[1], s.small_g_r.at[1]),
    ]
    big_g = [
        [
            Gather(
                lambda o, q=up(x, by): s.text.at[o, q, c, :, halves[0]], y, at_y,
                s.big_g_s.at[0, up(x, by)], s.big_g_r.at[0, up(x, by)],
            )
            for by in range(N)
        ],
        [
            Gather(
                lambda o, q=up(y, by): s.text.at[q, o, c, :, halves[1]], x, at_x,
                s.big_g_s.at[1, up(y, by)], s.big_g_r.at[1, up(y, by)],
            )
            for by in range(N)
        ],
    ]

    def core_block(h, by, core):
        if h == 0:
            return s.text.at[:, up(x, by), core, :, halves[0]]
        return s.text.at[up(y, by), :, core, :, halves[1]]

    def share(by):
        for h in range(2):
            for other in (1, 3, 2):
                big_g[h][by].wait(other)
            q = up(x, by) if h == 0 else up(y, by)
            block = core_block(h, by, c)
            send(block, block, s.core_g_s.at[h, q], s.core_g_r.at[h, q], other_core)

    own_image.wait()
    for reach in (3, 1):
        for way in range(2):
            z_send(way, 0, reach)
    own_text.wait()
    for h in range(2):
        small_g[h].start()
    for h in range(2):
        big_g[h][0].start()
    for by in (1, 3, 2):
        for h in range(2):
            small_g[h].wait(by)
            big_g[h][by].start()
    for way in range(2):
        z_wait(way, 3)
        for reach in (6, 4, 2):
            z_send(way, 3, reach)
    share(0)
    share(1)
    for way in range(2):
        z_wait(way, 6)
        for reach in (8, 7, 5):
            z_send(way, 6, reach)
    share(3)
    share(2)
    for by in (0, 1, 3, 2):
        for h in range(2):
            q = up(x, by) if h == 0 else up(y, by)
            arrive(core_block(h, by, 1 - c), s.core_g_s.at[h, q], s.core_g_r.at[h, q], other_core)
    for steps in (1, 2):
        for way in range(2):
            z_wait(way, steps)

    row_place = lax.broadcasted_iota(jnp.int32, (STRIP, COLS), 0)

    def diagonal(q, strip):
        first = y * 4096 + strip * 1024 + (q * N + x) * 64 + c * 32
        return row_place + first == s.col_ids[0:1, :]

    s.diag[...] = jnp.zeros((8, 128), F32)

    def chunk_stats(by):
        q = lax.rem(zh + by, N)
        images = s.image[pl.ds(q * N, N)].reshape(CHUNK, D)
        s.col_exp[q] = LOGIT_SCALE * lax.dot_general(
            images, s.text[...].reshape(COLS, D), (((1,), (1,)), ((), ())), preferred_element_type=F32
        )
        col_peak = None
        for strip in range(N):
            rows = slice(strip * STRIP, (strip + 1) * STRIP)
            logits = s.col_exp[q, rows, :]
            peak = jnp.max(logits, axis=1, keepdims=True)
            exps = jnp.exp(logits - peak)
            s.row_exp[q, rows, :] = exps
            s.row_peak[q, rows, :] = jnp.broadcast_to(peak, (STRIP, 128))
            log = peak + jnp.log(jnp.sum(exps, axis=1, keepdims=True))
            s.row_log[rows, :] = jnp.broadcast_to(log, (STRIP, 128))
            part = jnp.max(logits.reshape(STRIP // 8, 8, COLS), axis=0)
            col_peak = part if col_peak is None else jnp.maximum(col_peak, part)
        col_peak = jnp.max(col_peak, axis=0, keepdims=True)
        col_total = jnp.zeros((8, COLS), F32)
        diag = jnp.zeros((8, COLS), F32)
        for strip in range(N):
            rows = slice(strip * STRIP, (strip + 1) * STRIP)
            logits = s.col_exp[q, rows, :]
            exps = jnp.exp(logits - col_peak)
            s.col_exp[q, rows, :] = exps
            col_total = col_total + jnp.sum(exps.reshape(STRIP // 8, 8, COLS), axis=0)
            kept = jnp.where(diagonal(q, strip), logits, 0.0)
            diag = diag + jnp.sum(kept.reshape(STRIP // 8, 8, COLS), axis=0)
        s.diag[...] += sum(diag[:, j * 128 : (j + 1) * 128] for j in range(COLS // 128))
        s.col_peak[q] = jnp.broadcast_to(col_peak, (8, COLS))
        col_log = col_peak + jnp.log(jnp.sum(col_total, axis=0, keepdims=True))
        s.col_log[q] = jnp.broadcast_to(col_log, (8, COLS))
        dense = jnp.sum(jnp.where(eye(), s.row_log[...], 0.0), axis=0, keepdims=True)
        s.row_dense[q] = jnp.broadcast_to(dense, (8, 128))

    chunk_stats(0)
    for steps in (4, 5, 7):
        for way in range(2):
            z_wait(way, steps)

    def near_chunk(k, carry):
        chunk_stats(1 + 2 * k)
        return carry

    lax.fori_loop(0, 2, near_chunk, 0)
    for way in range(2):
        z_wait(way, FAR)
    chunk_stats(2)

    s.row1[z] = jnp.concatenate([s.row_dense[j][0:1] for j in range(N)], axis=0)
    exchange(s.row1, z, NZ, at_z, s.row1_s, s.row1_r)
    col_local = log_sum([s.col_log[j] for j in range(N)])[0:1]
    s.col1[xc] = jnp.concatenate([col_local[:, j * 128 : (j + 1) * 128] for j in range(8)], axis=0)
    exchange(s.col1, xc, N * CORES, at_xc, s.col1_s, s.col1_r)
    s.col2[y] = log_sum(collect(s.col1, xc, N * CORES, at_xc, s.col1_s, s.col1_r))
    exchange(s.col2, y, N, at_y, s.col2_s, s.col2_r)
    col_lse = log_sum(collect(s.col2, y, N, at_y, s.col2_s, s.col2_r))
    wide_col = jnp.concatenate([col_lse[j : j + 1] for j in range(8)], axis=1)
    row_lse = log_sum(collect(s.row1, z, NZ, at_z, s.row1_s, s.row1_r))
    on = eye()
    for j in range(N):
        spread = jnp.where(on, jnp.broadcast_to(row_lse[j : j + 1], (128, 128)), 0.0)
        column = jnp.sum(spread, axis=1, keepdims=True)
        s.row_scale[j] = (0.5 * LOGIT_SCALE) * jnp.exp(s.row_peak[j] - column)

    def chunk_weights(q, carry):
        col_scale = (0.5 * LOGIT_SCALE) * jnp.exp(s.col_peak[q, 0:1, :] - wide_col)
        for strip in range(N):
            rows = slice(strip * STRIP, (strip + 1) * STRIP)
            row_scale = jnp.concatenate([s.row_scale[q, rows, :]] * (COLS // 128), axis=1)
            value = s.row_exp[q, rows, :] * row_scale + s.col_exp[q, rows, :] * col_scale
            value = value - jnp.where(diagonal(q, strip), LOGIT_SCALE, 0.0)
            s.weights[q, rows, :] = value.astype(BF16)
        return carry

    lax.fori_loop(0, N, chunk_weights, 0)

    def grad_image(by):
        q = up(zh, by)
        out = jnp.dot(s.weights[q], s.text[...].reshape(COLS, D), preferred_element_type=F32)
        s.part_image[pl.ds(q * N, N)] = out.astype(BF16).reshape(N, ROWS, D)

    def z_part(way, steps):
        return s.part_image.at[up(z, -steps if way == 0 else steps, NZ)]

    def z_give(steps, target):
        for way in range(2):
            block, there = z_part(way, steps), s.z_in.at[way, steps]
            if steps == FAR:
                block, there = block.at[ends[way]], there.at[ends[way]]
            send(block, there, s.zs_s.at[way, steps], s.zs_r.at[way, steps], along(way, -target))

    def z_take(way, steps):
        got = s.z_in.at[way, steps]
        if steps == FAR:
            got = got.at[ends[way]]
        arrive(got, s.zs_s.at[way, steps], s.zs_r.at[way, steps], along(way, 1))

    def z_hub(way, steps, parts):
        total = z_part(way, steps)[...].astype(F32)
        for part in parts:
            z_take(way, part)
        for part in parts:
            if part != FAR:
                total = total + s.z_in[way, part].astype(F32)
        out = s.z_out.at[way, steps // 3 - 1]
        out[...] = total.astype(BF16)
        if FAR in parts:
            out[ends[way]] = (total[ends[way].start : ends[way].start + ends[way].size] + s.z_in[way, FAR, ends[way]].astype(F32)).astype(BF16)
        send(out, s.z_in.at[way, steps], s.zs_s.at[way, steps], s.zs_r.at[way, steps], along(way, -3))

    def z_last():
        total = s.part_image[z].astype(F32)
        for steps in (1, 3):
            for way in range(2):
                z_take(way, steps)
                total = total + s.z_in[way, steps].astype(F32)
        gi_out[...] = total.astype(BF16)

    def grad_text(by):
        place = up(y, by)
        wide = N * CORES * ROWS
        columns = pl.ds(pl.multiple_of(place * wide, wide), wide)
        w = s.weights[:, :, columns].reshape(N * CHUNK, wide)
        out = lax.dot_general(
            w, s.image[...].reshape(NZ * ROWS, D), (((0,), (0,)), ((), ())), preferred_element_type=F32
        )
        s.part_text[place] = out.astype(BF16).reshape(N, CORES, ROWS, D)
        send(s.part_text.at[place, :, 1 - c], s.part_core.at[place], s.core_s_s.at[by], s.core_s_r.at[by], other_core)

    def add_core(by):
        place = up(y, by)
        arrive(s.part_core.at[place], s.core_s_s.at[by], s.core_s_r.at[by], other_core)
        s.plane[place] = add(s.part_text[place, :, c], s.part_core[place])

    big_s = [
        [
            Scatter(
                lambda o, q=up(x, by): s.plane.at[o, q, :, halves[0]], s.big_in.at[0, up(x, by)], y, at_y,
                s.big_s_s.at[0, up(x, by)], s.big_s_r.at[0, up(x, by)],
            )
            for by in range(N)
        ],
        [
            Scatter(
                lambda o, q=up(y, by): s.plane.at[q, o, :, halves[1]], s.big_in.at[1, up(y, by)], x, at_x,
                s.big_s_s.at[1, up(y, by)], s.big_s_r.at[1, up(y, by)],
            )
            for by in range(N)
        ],
    ]
    small_s = [
        Scatter(lambda o: s.line.at[0, o], s.small_in.at[0], x, at_x, s.small_s_s.at[0], s.small_s_r.at[0]),
        Scatter(lambda o: s.line.at[1, o], s.small_in.at[1], y, at_y, s.small_s_s.at[1], s.small_s_r.at[1]),
    ]

    def fold(by):
        for h in range(2):
            q = up(x, by) if h == 0 else up(y, by)
            s.line[h, q] = big_s[h][by].finish()

    grad_image(2)
    z_give(8, 2)
    grad_image(1)
    grad_image(3)
    z_give(7, 1)
    z_give(5, -1)
    z_give(4, 1)
    grad_image(0)
    z_give(2, -1)
    z_give(1, 1)
    for by in (2, 1, 3, 0):
        grad_text(by)
    for way in range(2):
        z_hub(way, 6, (5, 7, 8))

    share_rows = jnp.sum(row_lse) * (1.0 / NZ)
    share_cols = jnp.sum(col_lse) * (1.0 / (N * N * CORES))
    own_share = share_rows + share_cols - 2.0 * jnp.sum(s.diag[...])
    s.loss1[xc] = jnp.full((1, 128), own_share, F32)
    exchange(s.loss1, xc, N * CORES, at_xc, s.loss1_s, s.loss1_r)

    for by in (2, 1, 3, 0):
        add_core(by)
        big_s[1][by].start()
    for by in (2, 1, 3, 0):
        big_s[0][by].start()
    for way in range(2):
        z_hub(way, 3, (2, 4, 6))
    s.loss2[y] = sum(collect(s.loss1, xc, N * CORES, at_xc, s.loss1_s, s.loss1_r))
    exchange(s.loss2, y, N, at_y, s.loss2_s, s.loss2_r)
    for by in (2, 1, 3, 0):
        fold(by)
    for h in range(2):
        small_s[h].start()
    s.loss3[z] = sum(collect(s.loss2, y, N, at_y, s.loss2_s, s.loss2_r))
    exchange(s.loss3, z, NZ, at_z, s.loss3_s, s.loss3_r)
    for h in range(2):
        gt_out[0, :, halves[h]] = small_s[h].finish()
    z_last()
    total = sum(collect(s.loss3, z, NZ, at_z, s.loss3_s, s.loss3_r))
    loss_out[0, 0] = jnp.max(total) / (2.0 * PAIRS)

    for copy in sent:
        copy.wait_send()


def per_device(images, texts):
    loss, grad_images, grad_texts = pl.pallas_call(
        kernel,
        out_shape=(
            jax.ShapeDtypeStruct((1, 1), F32),
            jax.ShapeDtypeStruct((ROWS, D), BF16),
            jax.ShapeDtypeStruct((1, ROWS, D), BF16),
        ),
        in_specs=[pl.BlockSpec(memory_space=pl.ANY)] * 2,
        out_specs=(
            pl.BlockSpec(memory_space=pltpu.SMEM),
            pl.BlockSpec(memory_space=pltpu.VMEM),
            pl.BlockSpec(memory_space=pltpu.VMEM),
        ),
        scratch_shapes=list(SCRATCH.values()),
        compiler_params=pltpu.CompilerParams(
            collective_id=0, has_side_effects=True, vmem_limit_bytes=48 * 1024 * 1024
        ),
        name="contrastive",
    )(images, texts)
    return loss.reshape(()), grad_images, grad_texts


def solution(mesh):
    in_specs = (P(("img", "txt"), None), P("img", "txt", None))
    out_specs = (P(), P(("img", "txt"), None), P("img", "txt", None))
    return jax.shard_map(
        per_device, mesh=mesh, in_specs=in_specs, out_specs=out_specs, check_vma=False
    )
```

```python
import jax
import jax.numpy as jnp
from jax import lax
from jax.experimental import pallas as pl
from jax.experimental.pallas import tpu as pltpu
from jax.sharding import PartitionSpec as P

LOGIT_SCALE = 1.0 / 0.07
MESH = pl.DeviceIdType.MESH
F32 = jnp.float32
BF16 = jnp.bfloat16

N = 4
NZ = 16
CORES = 2
ROWS = 32
D = 1024
WIDE = D // 2
CHUNK = N * ROWS
COLS = N * N * CORES * ROWS
PAIRS = 16384
STRIP = ROWS
FAR = NZ // 2

def dma(*shape):
    return pltpu.SemaphoreType.DMA(shape)


def bf16(*shape):
    return pltpu.VMEM(shape, BF16)


def f32(*shape):
    return pltpu.VMEM(shape, F32)


SCRATCH = dict(
    image=bf16(NZ, ROWS, D),
    text=bf16(N, N, CORES, ROWS, D),
    row_exp=f32(N, CHUNK, COLS),
    col_exp=f32(N, CHUNK, COLS),
    row_peak=f32(N, CHUNK, 128),
    row_scale=f32(N, CHUNK, 128),
    row_log=f32(CHUNK, 128),
    row_dense=f32(N, 8, 128),
    col_peak=f32(N, 8, COLS),
    col_log=f32(N, 8, COLS),
    col_ids=pltpu.VMEM((8, COLS), jnp.int32),
    diag=f32(8, 128),
    weights=bf16(N, CHUNK, COLS),
    part_image=bf16(NZ, ROWS, D),
    z_in=bf16(2, FAR + 1, ROWS, D),
    z_out=bf16(2, 2, ROWS, D),
    part_text=bf16(N, N, CORES, ROWS, D),
    part_core=bf16(N, N, ROWS, D),
    plane=bf16(N, N, ROWS, D),
    big_in=bf16(2, N, N, ROWS, WIDE),
    line=bf16(2, N, ROWS, WIDE),
    small_in=bf16(2, N, ROWS, WIDE),
    row1=f32(NZ, N, 128),
    col1=f32(N * CORES, 8, 128),
    col2=f32(N, 8, 128),
    loss1=f32(N * CORES, 1, 128),
    loss2=f32(N, 1, 128),
    loss3=f32(NZ, 1, 128),
    local_sem=dma(2),
    zg_s=dma(1), zg_r=dma(6),
    text_s=dma(1), small_g_r=dma(2, N), big_g_r=dma(2, N),
    core_g_s=dma(1), core_g_r=dma(1),
    row1_s=dma(1), row1_r=dma(1),
    col1_s=dma(1), col1_r=dma(1),
    col2_s=dma(1), col2_r=dma(1),
    loss1_s=dma(1), loss1_r=dma(1),
    loss2_s=dma(1), loss2_r=dma(1),
    loss3_s=dma(1), loss3_r=dma(1),
    core_s_s=dma(1), core_s_r=dma(N),
    zs_s=dma(1), zs_r=dma(5),
    plane_s=dma(1), big_s_r=dma(2, N), small_s_r=dma(2),
)
NAMES = list(SCRATCH)


class Refs:
    def __init__(self, refs):
        for name, ref in zip(NAMES, refs):
            setattr(self, name, ref)


def log_sum(parts):
    peak = parts[0]
    for part in parts[1:]:
        peak = jnp.maximum(peak, part)
    total = jnp.exp(parts[0] - peak)
    for part in parts[1:]:
        total = total + jnp.exp(part - peak)
    return peak + jnp.log(total)


def eye():
    rows = lax.broadcasted_iota(jnp.int32, (128, 128), 0)
    cols = lax.broadcasted_iota(jnp.int32, (128, 128), 1)
    return rows == cols


def add(a, b):
    return (a.astype(F32) + b.astype(F32)).astype(BF16)


def kernel(img_hbm, txt_hbm, loss_out, gi_out, gt_out, *refs):
    s = Refs(refs)
    img, txt = lax.axis_index("img"), lax.axis_index("txt")
    y, zl = img // N, lax.rem(img, N)
    zh, xc = txt // (N * CORES), lax.rem(txt, N * CORES)
    x, c = xc // CORES, lax.rem(xc, CORES)
    z = zh * N + zl

    def up(place, by, count=N):
        return lax.rem(place + (by + count) % count, count)

    def at_x(place):
        return (img, (zh * N + place) * CORES + c)

    def at_xc(place):
        return (img, zh * (N * CORES) + place)

    def at_y(place):
        return (place * N + zl, txt)

    def at_z(place):
        return (y * N + lax.rem(place, N), (place // N) * (N * CORES) + xc)

    other_core = (img, (zh * N + x) * CORES + (1 - c))

    own_image = pltpu.make_async_copy(img_hbm, s.image.at[z], s.local_sem.at[0])
    own_text = pltpu.make_async_copy(txt_hbm.at[0], s.text.at[y, x, c], s.local_sem.at[1])
    own_image.start()
    own_text.start()

    barrier = pltpu.get_barrier_semaphore()
    partners = [at_z(up(z, by, NZ)) for by in (3, -3, 2, -2, 1, -1)]
    partners += [at_y(up(y, by)) for by in range(1, N)] + [at_x(up(x, by)) for by in range(1, N)]
    partners += [other_core]
    for partner in partners:
        pl.semaphore_signal(barrier, inc=1, device_id=partner, device_id_type=MESH)
    lane = lax.broadcasted_iota(jnp.int32, (8, COLS), 1)
    s.col_ids[...] = (
        zh * 4096 + lax.rem(lane // 64, 4) * 1024 + lax.rem(lane // 32, 2) * 512
        + (lane // 256) * 128 + zl * 32 + lax.rem(lane, 32)
    )
    pl.semaphore_wait(barrier, len(partners))


    def remote(src, dst, send_sem, recv_sem, device):
        return pltpu.make_async_remote_copy(
            src_ref=src, dst_ref=dst, send_sem=send_sem, recv_sem=recv_sem,
            device_id=device, device_id_type=MESH,
        )

    def send(*args):
        remote(*args).start()

    def wait_bytes(ref, sem):
        pltpu.make_async_copy(ref, ref, sem).wait()

    def exchange(buf, me, count, device, ss, rs):
        for by in sorted(range(1, count), key=lambda k: -min(k, count - k)):
            send(buf.at[me], buf.at[me], ss.at[0], rs.at[0], device(up(me, by, count)))

    def collect(buf, count, ss, rs):
        wait_bytes(buf.at[pl.ds(0, count - 1)], rs.at[0])
        wait_bytes(buf.at[pl.ds(0, count - 1)], ss.at[0])
        return [buf[j] for j in range(count)]

    class Gather:
        def __init__(self, slot, me, device, ss, rs):
            self.slot, self.me, self.device, self.ss, self.rs = slot, me, device, ss, rs

        def start(self):
            own = self.slot(self.me)
            for by in (2, 1, 3):
                send(own, own, self.ss, self.rs(by), self.device(up(self.me, by)))

        def wait(self, by):
            wait_bytes(self.slot(up(self.me, by)), self.rs(N - by))

    class Scatter:
        def __init__(self, slot, r, me, device, ss, rs):
            self.slot, self.r = slot, r
            self.me, self.device, self.ss, self.rs = me, device, ss, rs

        def start(self):
            for by in (2, 1, 3):
                to = up(self.me, by)
                send(self.slot(to), self.r.at[by], self.ss, self.rs, self.device(to))

        def finish(self):
            wait_bytes(self.r.at[pl.ds(1, 3)], self.rs)
            total = self.slot(self.me)[...].astype(F32)
            for by in (1, 3, 2):
                total = total + self.r[by].astype(F32)
            return total.astype(BF16)

    ends = [pl.ds(0, ROWS // 2), pl.ds(ROWS // 2, ROWS // 2)]

    def along(way, steps):
        return at_z(up(z, steps if way == 0 else -steps, NZ))

    def z_sem(way, reach):
        return s.zg_r.at[{3: way, 6: 2 + way, 1: 4, 2: 4}.get(reach, 5)]

    def z_send(way, held, reaches):
        for reach in reaches:
            block = s.image.at[up(z, -held if way == 0 else held, NZ)]
            if reach == FAR:
                block = block.at[ends[way]]
            send(block, block, s.zg_s.at[0], z_sem(way, reach), along(way, reach - held))

    halves = [pl.ds(0, WIDE), pl.ds(WIDE, WIDE)]
    small_g = [
        Gather(lambda o: s.text.at[y, o, c, :, halves[0]], x, at_x, s.text_s.at[0], lambda k: s.small_g_r.at[0, k]),
        Gather(lambda o: s.text.at[o, x, c, :, halves[1]], y, at_y, s.text_s.at[0], lambda k: s.small_g_r.at[1, k]),
    ]
    big_g = [
        [
            Gather(
                lambda o, q=up(x, by): s.text.at[o, q, c, :, halves[0]], y, at_y,
                s.text_s.at[0], lambda k, q=up(x, by): s.big_g_r.at[0, q],
            )
            for by in range(N)
        ],
        [
            Gather(
                lambda o, q=up(y, by): s.text.at[q, o, c, :, halves[1]], x, at_x,
                s.text_s.at[0], lambda k, q=up(y, by): s.big_g_r.at[1, q],
            )
            for by in range(N)
        ],
    ]

    def core_block(h, by, core):
        if h == 0:
            return s.text.at[:, up(x, by), core, :, halves[0]]
        return s.text.at[up(y, by), :, core, :, halves[1]]

    def share(by):
        for h in range(2):
            wait_bytes(s.line.at[h, pl.ds(0, 3)], s.big_g_r.at[h, up(x, by) if h == 0 else up(y, by)])
            block = core_block(h, by, c)
            send(block, block, s.core_g_s.at[0], s.core_g_r.at[0], other_core)

    own_image.wait()
    for reach in (3, 1):
        for way in range(2):
            z_send(way, 0, (reach,))
    own_text.wait()
    for h in range(2):
        small_g[h].start()
    for h in range(2):
        big_g[h][0].start()
    for by in (1, 3, 2):
        for h in range(2):
            small_g[h].wait(by)
            big_g[h][by].start()
    one = s.image.at[0]
    for way in range(2):
        wait_bytes(one, z_sem(way, 3))
        z_send(way, 3, (6, 4, 2))
    share(0)
    for way in range(2):
        wait_bytes(one, z_sem(way, 6))
        z_send(way, 6, (8, 7, 5))
    share(1)
    share(3)
    share(2)
    wait_bytes(s.image, s.core_g_r.at[0])
    wait_bytes(s.image.at[pl.ds(0, 4)], z_sem(0, 1))

    row_place = lax.broadcasted_iota(jnp.int32, (STRIP, COLS), 0)

    def diagonal(q, strip):
        first = y * 4096 + strip * 1024 + (q * N + x) * 64 + c * 32
        return row_place + first == s.col_ids[0:1, :]

    s.diag[...] = jnp.zeros((8, 128), F32)

    def chunk_stats(by):
        q = lax.rem(zh + by, N)
        images = s.image[pl.ds(q * N, N)].reshape(CHUNK, D)
        s.col_exp[q] = LOGIT_SCALE * lax.dot_general(
            images, s.text[...].reshape(COLS, D), (((1,), (1,)), ((), ())), preferred_element_type=F32
        )
        col_peak = None
        for strip in range(N):
            rows = slice(strip * STRIP, (strip + 1) * STRIP)
            logits = s.col_exp[q, rows, :]
            peak = jnp.max(logits, axis=1, keepdims=True)
            exps = jnp.exp(logits - peak)
            s.row_exp[q, rows, :] = exps
            s.row_peak[q, rows, :] = jnp.broadcast_to(peak, (STRIP, 128))
            log = peak + jnp.log(jnp.sum(exps, axis=1, keepdims=True))
            s.row_log[rows, :] = jnp.broadcast_to(log, (STRIP, 128))
            part = jnp.max(logits.reshape(STRIP // 8, 8, COLS), axis=0)
            col_peak = part if col_peak is None else jnp.maximum(col_peak, part)
        col_peak = jnp.max(col_peak, axis=0, keepdims=True)
        col_total = jnp.zeros((8, COLS), F32)
        diag = jnp.zeros((8, COLS), F32)
        for strip in range(N):
            rows = slice(strip * STRIP, (strip + 1) * STRIP)
            logits = s.col_exp[q, rows, :]
            exps = jnp.exp(logits - col_peak)
            s.col_exp[q, rows, :] = exps
            col_total = col_total + jnp.sum(exps.reshape(STRIP // 8, 8, COLS), axis=0)
            kept = jnp.where(diagonal(q, strip), logits, 0.0)
            diag = diag + jnp.sum(kept.reshape(STRIP // 8, 8, COLS), axis=0)
        s.diag[...] += sum(diag[:, j * 128 : (j + 1) * 128] for j in range(COLS // 128))
        s.col_peak[q] = jnp.broadcast_to(col_peak, (8, COLS))
        col_log = col_peak + jnp.log(jnp.sum(col_total, axis=0, keepdims=True))
        s.col_log[q] = jnp.broadcast_to(col_log, (8, COLS))
        dense = jnp.sum(jnp.where(eye(), s.row_log[...], 0.0), axis=0, keepdims=True)
        s.row_dense[q] = jnp.broadcast_to(dense, (8, 128))

    chunk_stats(0)
    wait_bytes(s.image.at[pl.ds(0, 7)], z_sem(0, 4))

    def near_chunk(k, carry):
        chunk_stats(1 + k)
        return carry

    lax.fori_loop(0, 3, near_chunk, 0)

    s.row1[z] = jnp.concatenate([s.row_dense[j][0:1] for j in range(N)], axis=0)
    exchange(s.row1, z, NZ, at_z, s.row1_s, s.row1_r)
    col_local = log_sum([s.col_log[j] for j in range(N)])[0:1]
    s.col1[xc] = jnp.concatenate([col_local[:, j * 128 : (j + 1) * 128] for j in range(8)], axis=0)
    exchange(s.col1, xc, N * CORES, at_xc, s.col1_s, s.col1_r)
    s.col2[y] = log_sum(collect(s.col1, N * CORES, s.col1_s, s.col1_r))
    exchange(s.col2, y, N, at_y, s.col2_s, s.col2_r)
    col_lse = log_sum(collect(s.col2, N, s.col2_s, s.col2_r))
    wide_col = jnp.concatenate([col_lse[j : j + 1] for j in range(8)], axis=1)
    row_lse = log_sum(collect(s.row1, NZ, s.row1_s, s.row1_r))
    on = eye()
    for j in range(N):
        spread = jnp.where(on, jnp.broadcast_to(row_lse[j : j + 1], (128, 128)), 0.0)
        column = jnp.sum(spread, axis=1, keepdims=True)
        s.row_scale[j] = (0.5 * LOGIT_SCALE) * jnp.exp(s.row_peak[j] - column)

    def chunk_weights(q, carry):
        col_scale = (0.5 * LOGIT_SCALE) * jnp.exp(s.col_peak[q, 0:1, :] - wide_col)
        for strip in range(N):
            rows = slice(strip * STRIP, (strip + 1) * STRIP)
            row_scale = jnp.concatenate([s.row_scale[q, rows, :]] * (COLS // 128), axis=1)
            value = s.row_exp[q, rows, :] * row_scale + s.col_exp[q, rows, :] * col_scale
            value = value - jnp.where(diagonal(q, strip), LOGIT_SCALE, 0.0)
            s.weights[q, rows, :] = value.astype(BF16)
        return carry

    lax.fori_loop(0, N, chunk_weights, 0)

    def grad_image(by):
        q = up(zh, by)
        out = jnp.dot(s.weights[q], s.text[...].reshape(COLS, D), preferred_element_type=F32)
        s.part_image[pl.ds(q * N, N)] = out.astype(BF16).reshape(N, ROWS, D)

    def z_part(way, steps):
        return s.part_image.at[up(z, -steps if way == 0 else steps, NZ)]

    def zs_sem(way, steps):
        return s.zs_r.at[4 if steps in (1, 3) else (way if steps in (5, 7, 8) else 2 + way)]

    def z_give(steps, target):
        for way in range(2):
            block, there = z_part(way, steps), s.z_in.at[way, steps]
            if steps == FAR:
                block, there = block.at[ends[way]], there.at[ends[way]]
            send(block, there, s.zs_s.at[0], zs_sem(way, steps), along(way, -target))

    def z_hub(way, steps, parts):
        waited = s.image.at[pl.ds(0, 5), ends[0]] if FAR in parts else s.image.at[pl.ds(0, 3)]
        wait_bytes(waited, zs_sem(way, parts[0]))
        out = s.z_out.at[way, steps // 3 - 1]
        for p in range(2):
            total = z_part(way, steps)[ends[p]].astype(F32)
            for part in parts:
                if part != FAR or p == way:
                    total = total + s.z_in[way, part, ends[p]].astype(F32)
            out[ends[p]] = total.astype(BF16)
        send(out, s.z_in.at[way, steps], s.zs_s.at[0], zs_sem(way, steps), along(way, -3))

    def z_last():
        wait_bytes(s.image.at[pl.ds(0, 4)], zs_sem(0, 1))
        total = s.part_image[z].astype(F32)
        for steps in (1, 3):
            for way in range(2):
                total = total + s.z_in[way, steps].astype(F32)
        gi_out[...] = total.astype(BF16)

    def grad_text(by):
        place = up(y, by)
        wide = N * CORES * ROWS
        columns = pl.ds(pl.multiple_of(place * wide, wide), wide)
        w = s.weights[:, :, columns].reshape(N * CHUNK, wide)
        out = lax.dot_general(
            w, s.image[...].reshape(NZ * ROWS, D), (((0,), (0,)), ((), ())), preferred_element_type=F32
        )
        s.part_text[place] = out.astype(BF16).reshape(N, CORES, ROWS, D)
        send(s.part_text.at[place, :, 1 - c], s.part_core.at[place], s.core_s_s.at[0], s.core_s_r.at[by], other_core)

    def add_core(by):
        place = up(y, by)
        wait_bytes(s.part_core.at[place], s.core_s_r.at[by])
        s.plane[place] = add(s.part_text[place, :, c], s.part_core[place])

    big_s = [
        [
            Scatter(
                lambda o, q=up(x, by): s.plane.at[o, q, :, halves[0]], s.big_in.at[0, up(x, by)], y, at_y,
                s.plane_s.at[0], s.big_s_r.at[0, up(x, by)],
            )
            for by in range(N)
        ],
        [
            Scatter(
                lambda o, q=up(y, by): s.plane.at[q, o, :, halves[1]], s.big_in.at[1, up(y, by)], x, at_x,
                s.plane_s.at[0], s.big_s_r.at[1, up(y, by)],
            )
            for by in range(N)
        ],
    ]
    small_s = [
        Scatter(lambda o: s.line.at[0, o], s.small_in.at[0], x, at_x, s.plane_s.at[0], s.small_s_r.at[0]),
        Scatter(lambda o: s.line.at[1, o], s.small_in.at[1], y, at_y, s.plane_s.at[0], s.small_s_r.at[1]),
    ]

    def fold(by):
        for h in range(2):
            q = up(x, by) if h == 0 else up(y, by)
            s.line[h, q] = big_s[h][by].finish()

    grad_image(2)
    z_give(8, 2)
    grad_image(1)
    grad_image(3)
    z_give(7, 1)
    z_give(5, -1)
    z_give(4, 1)
    grad_image(0)
    z_give(2, -1)
    for by in (2, 1, 3, 0):
        grad_text(by)
    z_give(1, 1)

    share_rows = jnp.sum(row_lse) * (1.0 / NZ)
    share_cols = jnp.sum(col_lse) * (1.0 / (N * N * CORES))
    own_share = share_rows + share_cols - 2.0 * jnp.sum(s.diag[...])
    s.loss3[z] = jnp.full((1, 128), own_share, F32)
    exchange(s.loss3, z, NZ, at_z, s.loss3_s, s.loss3_r)

    for by in (2, 1, 3, 0):
        add_core(by)
        big_s[1][by].start()
    for by in (2, 1, 3, 0):
        big_s[0][by].start()
    for way in range(2):
        z_hub(way, 6, (5, 7, 8))
    s.loss1[xc] = sum(collect(s.loss3, NZ, s.loss3_s, s.loss3_r))
    exchange(s.loss1, xc, N * CORES, at_xc, s.loss1_s, s.loss1_r)
    for by in (2, 1, 3, 0):
        fold(by)
    for h in range(2):
        small_s[h].start()
    for way in range(2):
        z_hub(way, 3, (2, 4, 6))
    s.loss2[y] = sum(collect(s.loss1, N * CORES, s.loss1_s, s.loss1_r))
    exchange(s.loss2, y, N, at_y, s.loss2_s, s.loss2_r)
    for h in range(2):
        gt_out[0, :, halves[h]] = small_s[h].finish()
    total = sum(collect(s.loss2, N, s.loss2_s, s.loss2_r))
    loss_out[0, 0] = jnp.max(total) / (2.0 * PAIRS)
    z_last()

    fifteen = s.image.at[pl.ds(0, NZ - 1)]
    for sem in (s.zg_s, s.text_s, s.zs_s, s.plane_s):
        wait_bytes(fifteen, sem.at[0])
    for sem in (s.core_g_s, s.core_s_s):
        wait_bytes(s.image, sem.at[0])


def per_device(images, texts):
    loss, grad_images, grad_texts = pl.pallas_call(
        kernel,
        out_shape=(
            jax.ShapeDtypeStruct((1, 1), F32),
            jax.ShapeDtypeStruct((ROWS, D), BF16),
            jax.ShapeDtypeStruct((1, ROWS, D), BF16),
        ),
        in_specs=[pl.BlockSpec(memory_space=pl.ANY)] * 2,
        out_specs=(
            pl.BlockSpec(memory_space=pltpu.SMEM),
            pl.BlockSpec(memory_space=pltpu.VMEM),
            pl.BlockSpec(memory_space=pltpu.VMEM),
        ),
        scratch_shapes=list(SCRATCH.values()),
        compiler_params=pltpu.CompilerParams(
            collective_id=0, has_side_effects=True, vmem_limit_bytes=60 * 1024 * 1024
        ),
        name="contrastive",
    )(images, texts)
    return loss.reshape(()), grad_images, grad_texts


def solution(mesh):
    in_specs = (P(("img", "txt"), None), P("img", "txt", None))
    out_specs = (P(), P(("img", "txt"), None), P("img", "txt", None))
    return jax.shard_map(
        per_device, mesh=mesh, in_specs=in_specs, out_specs=out_specs, check_vma=False
    )
```

```python
import jax
import jax.numpy as jnp
from jax import lax
from jax.experimental import pallas as pl
from jax.experimental.pallas import tpu as pltpu
from jax.sharding import PartitionSpec as P

LOGIT_SCALE = 1.0 / 0.07
MESH = pl.DeviceIdType.MESH
F32 = jnp.float32
BF16 = jnp.bfloat16

N = 4
NZ = 16
CORES = 2
ROWS = 32
D = 1024
WIDE = D // 2
CHUNK = N * ROWS
COLS = N * N * CORES * ROWS
PAIRS = 16384
STRIP = ROWS
FAR = NZ // 2

PLACES = [0, 1, -1, 3, -3, 2, -2, 4, -4, 6, -6, 5, -5, 7, -7, 8]

def dma(*shape):
    return pltpu.SemaphoreType.DMA(shape)


def bf16(*shape):
    return pltpu.VMEM(shape, BF16)


def f32(*shape):
    return pltpu.VMEM(shape, F32)


SCRATCH = dict(
    image=bf16(NZ, ROWS, D),
    text=bf16(N, N, CORES, ROWS, D),
    row_exp=f32(N, CHUNK, COLS),
    col_exp=f32(N, CHUNK, COLS),
    row_peak=f32(N, CHUNK, 128),
    row_scale=f32(N, CHUNK, 128),
    row_dense=f32(N, 128),
    col_peak=f32(N, 8, COLS),
    col_log=f32(N, 8, COLS),
    col_ids=pltpu.VMEM((8, COLS), jnp.int32),
    diag=f32(8, 128),
    weights=bf16(N, CHUNK, COLS),
    part_image=bf16(NZ, ROWS, D),
    z_in=bf16(2, FAR + 1, ROWS, D),
    z_out=bf16(2, 2, ROWS, D),
    part_text=bf16(N, N, CORES, ROWS, D),
    part_core=bf16(N, N, ROWS, D),
    plane=bf16(N, N, ROWS, D),
    big_in=bf16(2, N, N, ROWS, WIDE),
    line=bf16(2, N, ROWS, WIDE),
    small_in=bf16(2, N, ROWS, WIDE),
    row1=f32(NZ, N, 128),
    col1=f32(N * CORES, 8, 128),
    col2=f32(N, 8, 128),
    loss1=f32(N * CORES, 1, 128),
    loss2=f32(N, 1, 128),
    loss3=f32(NZ, 1, 128),
    local_sem=dma(2),
    zg_s=dma(1), zg_r=dma(7),
    text_s=dma(1), small_g_r=dma(2, N), big_g_r=dma(2, N),
    core_g_s=dma(1), core_g_r=dma(1),
    row1_s=dma(1), row1_r=dma(1),
    col1_s=dma(1), col1_r=dma(1),
    col2_s=dma(1), col2_r=dma(1),
    loss1_s=dma(1), loss1_r=dma(1),
    loss2_s=dma(1), loss2_r=dma(1),
    loss3_s=dma(1), loss3_r=dma(1),
    core_s_s=dma(1), core_s_r=dma(N),
    zs_s=dma(1), zs_r=dma(5),
    plane_s=dma(1), big_s_r=dma(2, N), small_s_r=dma(2),
)
NAMES = list(SCRATCH)


class Refs:
    def __init__(self, refs):
        for name, ref in zip(NAMES, refs):
            setattr(self, name, ref)


def log_sum(parts):
    peak = parts[0]
    for part in parts[1:]:
        peak = jnp.maximum(peak, part)
    total = jnp.exp(parts[0] - peak)
    for part in parts[1:]:
        total = total + jnp.exp(part - peak)
    return peak + jnp.log(total)


def add(a, b):
    return (a.astype(F32) + b.astype(F32)).astype(BF16)


def kernel(img_hbm, txt_hbm, loss_out, both_out, *refs):
    s = Refs(refs)
    img, txt = lax.axis_index("img"), lax.axis_index("txt")
    y, zl = img // N, lax.rem(img, N)
    zh, xc = txt // (N * CORES), lax.rem(txt, N * CORES)
    x, c = xc // CORES, lax.rem(xc, CORES)
    z = zh * N + zl

    def up(place, by, count=N):
        return lax.rem(place + (by + count) % count, count)

    def at_x(place):
        return (img, (zh * N + place) * CORES + c)

    def at_xc(place):
        return (img, zh * (N * CORES) + place)

    def at_y(place):
        return (place * N + zl, txt)

    def at_z(place):
        return (y * N + lax.rem(place, N), (place // N) * (N * CORES) + xc)

    other_core = (img, (zh * N + x) * CORES + (1 - c))

    own_image = pltpu.make_async_copy(img_hbm, s.image.at[0], s.local_sem.at[0])
    own_text = pltpu.make_async_copy(txt_hbm.at[0], s.text.at[y, x, c], s.local_sem.at[1])
    own_image.start()
    own_text.start()

    barrier = pltpu.get_barrier_semaphore()
    partners = [at_z(up(z, by, NZ)) for by in (3, -3, 2, -2, 1, -1)]
    partners += [at_y(up(y, by)) for by in range(1, N)] + [at_x(up(x, by)) for by in range(1, N)]
    partners += [other_core]
    for partner in partners:
        pl.semaphore_signal(barrier, inc=1, device_id=partner, device_id_type=MESH)
    lane = lax.broadcasted_iota(jnp.int32, (8, COLS), 1)
    s.col_ids[...] = (
        zh * 4096 + lax.rem(lane // 64, 4) * 1024 + lax.rem(lane // 32, 2) * 512
        + (lane // 256) * 128 + zl * 32 + lax.rem(lane, 32)
    )
    pl.semaphore_wait(barrier, len(partners))


    def remote(src, dst, send_sem, recv_sem, device):
        return pltpu.make_async_remote_copy(
            src_ref=src, dst_ref=dst, send_sem=send_sem, recv_sem=recv_sem,
            device_id=device, device_id_type=MESH,
        )

    def send(*args):
        remote(*args).start()

    def wait_bytes(ref, sem):
        pltpu.make_async_copy(ref, ref, sem).wait()

    def exchange(buf, me, count, device, ss, rs):
        for by in sorted(range(1, count), key=lambda k: -min(k, count - k)):
            send(buf.at[me], buf.at[me], ss.at[0], rs.at[0], device(up(me, by, count)))

    def collect(buf, count, ss, rs):
        wait_bytes(buf.at[pl.ds(0, count - 1)], rs.at[0])
        wait_bytes(buf.at[pl.ds(0, count - 1)], ss.at[0])
        return [buf[j] for j in range(count)]

    class Gather:
        def __init__(self, slot, me, device, ss, rs):
            self.slot, self.me, self.device, self.ss, self.rs = slot, me, device, ss, rs

        def start(self):
            own = self.slot(self.me)
            for by in (2, 1, 3):
                send(own, own, self.ss, self.rs(by), self.device(up(self.me, by)))

        def wait(self, by):
            wait_bytes(self.slot(up(self.me, by)), self.rs(N - by))

    class Scatter:
        def __init__(self, slot, r, me, device, ss, rs):
            self.slot, self.r = slot, r
            self.me, self.device, self.ss, self.rs = me, device, ss, rs

        def start(self):
            for by in (2, 1, 3):
                to = up(self.me, by)
                send(self.slot(to), self.r.at[by], self.ss, self.rs, self.device(to))

        def finish(self):
            wait_bytes(self.r.at[pl.ds(1, 3)], self.rs)
            total = self.slot(self.me)[...].astype(F32)
            for by in (1, 3, 2):
                total = total + self.r[by].astype(F32)
            return total.astype(BF16)

    ends = [pl.ds(0, ROWS // 2), pl.ds(ROWS // 2, ROWS // 2)]

    def along(way, steps):
        return at_z(up(z, steps if way == 0 else -steps, NZ))

    def z_sem(way, reach):
        return s.zg_r.at[{3: way, 6: 2 + way, 1: 4, 2: 5, 4: 5}.get(reach, 6)]

    def slot(way, steps):
        return PLACES.index(steps if way == 1 or steps == FAR else -steps)

    def z_send(way, held, reaches):
        for reach in reaches:
            block, there = s.image.at[slot(way, held)], s.image.at[slot(way, reach)]
            if reach == FAR:
                block, there = block.at[ends[way]], there.at[ends[way]]
            send(block, there, s.zg_s.at[0], z_sem(way, reach), along(way, reach - held))

    halves = [pl.ds(0, WIDE), pl.ds(WIDE, WIDE)]
    small_g = [
        Gather(lambda o: s.text.at[y, o, c, :, halves[0]], x, at_x, s.text_s.at[0], lambda k: s.small_g_r.at[0, k]),
        Gather(lambda o: s.text.at[o, x, c, :, halves[1]], y, at_y, s.text_s.at[0], lambda k: s.small_g_r.at[1, k]),
    ]
    big_g = [
        [
            Gather(
                lambda o, q=up(x, by): s.text.at[o, q, c, :, halves[0]], y, at_y,
                s.text_s.at[0], lambda k, q=up(x, by): s.big_g_r.at[0, q],
            )
            for by in range(N)
        ],
        [
            Gather(
                lambda o, q=up(y, by): s.text.at[q, o, c, :, halves[1]], x, at_x,
                s.text_s.at[0], lambda k, q=up(y, by): s.big_g_r.at[1, q],
            )
            for by in range(N)
        ],
    ]

    def core_block(h, by, core):
        if h == 0:
            return s.text.at[:, up(x, by), core, :, halves[0]]
        return s.text.at[up(y, by), :, core, :, halves[1]]

    def share(by):
        for h in range(2):
            wait_bytes(s.line.at[h, pl.ds(0, 3)], s.big_g_r.at[h, up(x, by) if h == 0 else up(y, by)])
            block = core_block(h, by, c)
            send(block, block, s.core_g_s.at[0], s.core_g_r.at[0], other_core)

    own_image.wait()
    for reach in (3, 1):
        for way in range(2):
            z_send(way, 0, (reach,))
    own_text.wait()
    for h in range(2):
        small_g[h].start()
    for h in range(2):
        big_g[h][0].start()
    for by in (1, 3, 2):
        for h in range(2):
            small_g[h].wait(by)
            big_g[h][by].start()
    one = s.image.at[0]
    for way in range(2):
        wait_bytes(one, z_sem(way, 3))
        z_send(way, 3, (6, 4, 2))
    share(0)
    for way in range(2):
        wait_bytes(one, z_sem(way, 6))
        z_send(way, 6, (5, 7, 8))
    share(1)
    share(3)
    share(2)
    wait_bytes(s.image, s.core_g_r.at[0])

    row_place = lax.broadcasted_iota(jnp.int32, (STRIP, COLS), 0)

    def origin(g, strip):
        o = up(z, PLACES[g * N + strip], NZ)
        return o // N, lax.rem(o, N)

    def diagonal(g, strip):
        q, r = origin(g, strip)
        first = y * 4096 + r * 1024 + (q * N + x) * 64 + c * 32
        return row_place + first == s.col_ids[0:1, :]

    def in_lanes(g, strip):
        _, r = origin(g, strip)
        rows = lax.broadcasted_iota(jnp.int32, (STRIP, 128), 0)
        return rows + r * ROWS == lax.broadcasted_iota(jnp.int32, (STRIP, 128), 1)

    def in_rows(g, strip):
        q, _ = origin(g, strip)
        return lax.broadcasted_iota(jnp.int32, (N, 128), 0) == q

    s.row_dense[...] = jnp.zeros((N, 128), F32)
    s.diag[...] = jnp.zeros((8, 128), F32)

    def chunk_stats(q):
        images = s.image[q * N : (q + 1) * N].reshape(CHUNK, D)
        s.col_exp[q] = LOGIT_SCALE * lax.dot_general(
            images, s.text[...].reshape(COLS, D), (((1,), (1,)), ((), ())), preferred_element_type=F32
        )
        col_peak = None
        for strip in range(N):
            rows = slice(strip * STRIP, (strip + 1) * STRIP)
            logits = s.col_exp[q, rows, :]
            peak = jnp.max(logits, axis=1, keepdims=True)
            exps = jnp.exp(logits - peak)
            s.row_exp[q, rows, :] = exps
            s.row_peak[q, rows, :] = jnp.broadcast_to(peak, (STRIP, 128))
            log = peak + jnp.log(jnp.sum(exps, axis=1, keepdims=True))
            dense = jnp.sum(jnp.where(in_lanes(q, strip), log, 0.0), axis=0, keepdims=True)
            s.row_dense[...] += jnp.where(in_rows(q, strip), dense, 0.0)
            part = jnp.max(logits.reshape(STRIP // 8, 8, COLS), axis=0)
            col_peak = part if col_peak is None else jnp.maximum(col_peak, part)
        col_peak = jnp.max(col_peak, axis=0, keepdims=True)
        col_total = jnp.zeros((8, COLS), F32)
        diag = jnp.zeros((8, COLS), F32)
        for strip in range(N):
            rows = slice(strip * STRIP, (strip + 1) * STRIP)
            logits = s.col_exp[q, rows, :]
            exps = jnp.exp(logits - col_peak)
            s.col_exp[q, rows, :] = exps
            col_total = col_total + jnp.sum(exps.reshape(STRIP // 8, 8, COLS), axis=0)
            kept = jnp.where(diagonal(q, strip), logits, 0.0)
            diag = diag + jnp.sum(kept.reshape(STRIP // 8, 8, COLS), axis=0)
        s.diag[...] += sum(diag[:, j * 128 : (j + 1) * 128] for j in range(COLS // 128))
        s.col_peak[q] = jnp.broadcast_to(col_peak, (8, COLS))
        col_log = col_peak + jnp.log(jnp.sum(col_total, axis=0, keepdims=True))
        s.col_log[q] = jnp.broadcast_to(col_log, (8, COLS))

    wait_bytes(s.image.at[pl.ds(0, 2)], z_sem(0, 1))
    chunk_stats(0)
    wait_bytes(s.image.at[pl.ds(0, 4)], z_sem(0, 2))
    chunk_stats(1)
    wait_bytes(s.image.at[pl.ds(0, 5)], z_sem(0, 5))
    chunk_stats(2)
    chunk_stats(3)

    s.row1[z] = s.row_dense[...]
    exchange(s.row1, z, NZ, at_z, s.row1_s, s.row1_r)
    col_local = log_sum([s.col_log[j] for j in range(N)])[0:1]
    s.col1[xc] = jnp.concatenate([col_local[:, j * 128 : (j + 1) * 128] for j in range(8)], axis=0)
    exchange(s.col1, xc, N * CORES, at_xc, s.col1_s, s.col1_r)
    s.col2[y] = log_sum(collect(s.col1, N * CORES, s.col1_s, s.col1_r))
    exchange(s.col2, y, N, at_y, s.col2_s, s.col2_r)
    col_lse = log_sum(collect(s.col2, N, s.col2_s, s.col2_r))
    wide_col = jnp.concatenate([col_lse[j : j + 1] for j in range(8)], axis=1)
    row_lse = log_sum(collect(s.row1, NZ, s.row1_s, s.row1_r))
    for j in range(NZ):
        g, strip = j // N, j % N
        rows = slice(strip * STRIP, (strip + 1) * STRIP)
        lanes = jnp.sum(jnp.where(in_rows(g, strip), row_lse, 0.0), axis=0, keepdims=True)
        column = jnp.sum(jnp.where(in_lanes(g, strip), lanes, 0.0), axis=1, keepdims=True)
        s.row_scale[g, rows, :] = (0.5 * LOGIT_SCALE) * jnp.exp(s.row_peak[g, rows, :] - column)

    def chunk_weights(q):
        col_scale = (0.5 * LOGIT_SCALE) * jnp.exp(s.col_peak[q, 0:1, :] - wide_col)
        for strip in range(N):
            rows = slice(strip * STRIP, (strip + 1) * STRIP)
            row_scale = jnp.concatenate([s.row_scale[q, rows, :]] * (COLS // 128), axis=1)
            value = s.row_exp[q, rows, :] * row_scale + s.col_exp[q, rows, :] * col_scale
            value = value - jnp.where(diagonal(q, strip), LOGIT_SCALE, 0.0)
            s.weights[q, rows, :] = value.astype(BF16)

    for g in (3, 2, 1, 0):
        chunk_weights(g)

    def grad_image(g):
        out = jnp.dot(s.weights[g], s.text[...].reshape(COLS, D), preferred_element_type=F32)
        s.part_image[g * N : (g + 1) * N] = out.astype(BF16).reshape(N, ROWS, D)

    def z_part(way, steps):
        return s.part_image.at[slot(way, steps)]

    def zs_sem(way, steps):
        return s.zs_r.at[4 if steps in (1, 3) else (way if steps in (5, 7, 8) else 2 + way)]

    def z_give(steps, target):
        for way in range(2):
            block, there = z_part(way, steps), s.z_in.at[way, steps]
            if steps == FAR:
                block, there = block.at[ends[way]], there.at[ends[way]]
            send(block, there, s.zs_s.at[0], zs_sem(way, steps), along(way, -target))

    def z_hub(way, steps, parts):
        waited = s.image.at[pl.ds(0, 5), ends[0]] if FAR in parts else s.image.at[pl.ds(0, 3)]
        wait_bytes(waited, zs_sem(way, parts[0]))
        out = s.z_out.at[way, steps // 3 - 1]
        for p in range(2):
            total = z_part(way, steps)[ends[p]].astype(F32)
            for part in parts:
                if part != FAR or p == way:
                    total = total + s.z_in[way, part, ends[p]].astype(F32)
            out[ends[p]] = total.astype(BF16)
        send(out, s.z_in.at[way, steps], s.zs_s.at[0], zs_sem(way, steps), along(way, -3))

    def z_last():
        wait_bytes(s.image.at[pl.ds(0, 4)], zs_sem(0, 1))
        total = s.part_image[0].astype(F32)
        for steps in (1, 3):
            for way in range(2):
                total = total + s.z_in[way, steps].astype(F32)
        both_out[0] = total.astype(BF16)

    def grad_text(by):
        place = up(y, by)
        wide = N * CORES * ROWS
        columns = pl.ds(pl.multiple_of(place * wide, wide), wide)
        w = s.weights[:, :, columns].reshape(N * CHUNK, wide)
        out = lax.dot_general(
            w, s.image[...].reshape(NZ * ROWS, D), (((0,), (0,)), ((), ())), preferred_element_type=F32
        )
        s.part_text[place] = out.astype(BF16).reshape(N, CORES, ROWS, D)
        send(s.part_text.at[place, :, 1 - c], s.part_core.at[place], s.core_s_s.at[0], s.core_s_r.at[by], other_core)

    def add_core(by):
        place = up(y, by)
        wait_bytes(s.part_core.at[place], s.core_s_r.at[by])
        s.plane[place] = add(s.part_text[place, :, c], s.part_core[place])

    big_s = [
        [
            Scatter(
                lambda o, q=up(x, by): s.plane.at[o, q, :, halves[0]], s.big_in.at[0, up(x, by)], y, at_y,
                s.plane_s.at[0], s.big_s_r.at[0, up(x, by)],
            )
            for by in range(N)
        ],
        [
            Scatter(
                lambda o, q=up(y, by): s.plane.at[q, o, :, halves[1]], s.big_in.at[1, up(y, by)], x, at_x,
                s.plane_s.at[0], s.big_s_r.at[1, up(y, by)],
            )
            for by in range(N)
        ],
    ]
    small_s = [
        Scatter(lambda o: s.line.at[0, o], s.small_in.at[0], x, at_x, s.plane_s.at[0], s.small_s_r.at[0]),
        Scatter(lambda o: s.line.at[1, o], s.small_in.at[1], y, at_y, s.plane_s.at[0], s.small_s_r.at[1]),
    ]

    def fold(by):
        for h in range(2):
            q = up(x, by) if h == 0 else up(y, by)
            s.line[h, q] = big_s[h][by].finish()

    grad_image(3)
    z_give(8, 2)
    z_give(7, 1)
    grad_image(2)
    z_give(5, -1)
    grad_image(1)
    z_give(4, 1)
    z_give(2, -1)
    grad_image(0)
    for by in (2, 1, 3, 0):
        grad_text(by)
    z_give(1, 1)

    share_rows = jnp.sum(row_lse) * (1.0 / NZ)
    share_cols = jnp.sum(col_lse) * (1.0 / (N * N * CORES))
    own_share = share_rows + share_cols - 2.0 * jnp.sum(s.diag[...])
    s.loss3[z] = jnp.full((1, 128), own_share, F32)
    exchange(s.loss3, z, NZ, at_z, s.loss3_s, s.loss3_r)

    for by in (2, 1, 3, 0):
        add_core(by)
        big_s[1][by].start()
    for by in (2, 1, 3, 0):
        big_s[0][by].start()
    for way in range(2):
        z_hub(way, 6, (5, 7, 8))
    s.loss1[xc] = sum(collect(s.loss3, NZ, s.loss3_s, s.loss3_r))
    exchange(s.loss1, xc, N * CORES, at_xc, s.loss1_s, s.loss1_r)
    for by in (2, 1, 3, 0):
        fold(by)
    for h in range(2):
        small_s[h].start()
    for way in range(2):
        z_hub(way, 3, (2, 4, 6))
    s.loss2[y] = sum(collect(s.loss1, N * CORES, s.loss1_s, s.loss1_r))
    exchange(s.loss2, y, N, at_y, s.loss2_s, s.loss2_r)
    for h in range(2):
        both_out[1, :, halves[h]] = small_s[h].finish()
    total = sum(collect(s.loss2, N, s.loss2_s, s.loss2_r))
    loss_out[0, 0] = jnp.max(total) / (2.0 * PAIRS)
    z_last()

    fifteen = s.image.at[pl.ds(0, NZ - 1)]
    for sem in (s.zg_s, s.text_s, s.zs_s, s.plane_s):
        wait_bytes(fifteen, sem.at[0])
    for sem in (s.core_g_s, s.core_s_s):
        wait_bytes(s.image, sem.at[0])


def per_device(images, texts):
    loss, both = pl.pallas_call(
        kernel,
        out_shape=(
            jax.ShapeDtypeStruct((1, 1), F32),
            jax.ShapeDtypeStruct((2, ROWS, D), BF16),
        ),
        in_specs=[pl.BlockSpec(memory_space=pl.ANY)] * 2,
        out_specs=(
            pl.BlockSpec(memory_space=pltpu.SMEM),
            pl.BlockSpec(memory_space=pltpu.VMEM),
        ),
        scratch_shapes=list(SCRATCH.values()),
        compiler_params=pltpu.CompilerParams(
            collective_id=0, has_side_effects=True, vmem_limit_bytes=60 * 1024 * 1024
        ),
        name="contrastive",
    )(images, texts)
    return loss.reshape(()), both[0], both[1:2]


def solution(mesh):
    in_specs = (P(("img", "txt"), None), P("img", "txt", None))
    out_specs = (P(), P(("img", "txt"), None), P("img", "txt", None))
    return jax.shard_map(
        per_device, mesh=mesh, in_specs=in_specs, out_specs=out_specs, check_vma=False
    )
```

```python
import jax
import jax.numpy as jnp
from jax import lax
from jax.experimental import pallas as pl
from jax.experimental.pallas import tpu as pltpu
from jax.sharding import PartitionSpec as P

LOGIT_SCALE = 1.0 / 0.07
MESH = pl.DeviceIdType.MESH
F32 = jnp.float32
BF16 = jnp.bfloat16

N = 4
NZ = 16
CORES = 2
ROWS = 32
D = 1024
WIDE = D // 2
CHUNK = N * ROWS
COLS = N * N * CORES * ROWS
PAIRS = 16384
STRIP = ROWS
FAR = NZ // 2

PLACES = [0, 1, -1, 3, -3, 2, -2, 4, -4, 6, -6, 5, -5, 7, -7, 8]

def dma(*shape):
    return pltpu.SemaphoreType.DMA(shape)


def bf16(*shape):
    return pltpu.VMEM(shape, BF16)


def f32(*shape):
    return pltpu.VMEM(shape, F32)


SCRATCH = dict(
    image=bf16(NZ, ROWS, D),
    text=bf16(N, N, CORES, ROWS, D),
    row_exp=f32(N, CHUNK, COLS),
    col_exp=f32(N, CHUNK, COLS),
    row_peak=f32(N, CHUNK, 128),
    row_scale=f32(N, CHUNK, 128),
    row_dense=f32(N, 128),
    col_peak=f32(N, 8, COLS),
    col_log=f32(N, 8, COLS),
    col_ids=pltpu.VMEM((8, COLS), jnp.int32),
    diag=f32(8, 128),
    weights=bf16(N, CHUNK, COLS),
    part_image=bf16(NZ, ROWS, D),
    z_in=bf16(2, FAR + 1, ROWS, D),
    z_out=bf16(2, 2, ROWS, D),
    part_text=bf16(N, N, CORES, ROWS, D),
    part_core=bf16(N, N, ROWS, D),
    plane=bf16(N, N, ROWS, D),
    big_in=bf16(2, N, N, ROWS, WIDE),
    line=bf16(2, N, ROWS, WIDE),
    small_in=bf16(2, N, ROWS, WIDE),
    row1=f32(NZ, N, 128),
    col1=f32(N * CORES, 8, 128),
    col2=f32(N, 8, 128),
    loss1=f32(N * CORES, 1, 128),
    loss2=f32(N, 1, 128),
    loss3=f32(NZ, 1, 128),
    local_sem=dma(2),
    zg_s=dma(1), zg_r=dma(7),
    text_s=dma(1), small_g_r=dma(2, N), big_g_r=dma(2, N),
    core_g_s=dma(1), core_g_r=dma(1),
    row1_s=dma(1), row1_r=dma(1),
    col1_s=dma(1), col1_r=dma(1),
    col2_s=dma(1), col2_r=dma(1),
    loss1_s=dma(1), loss1_r=dma(1),
    loss2_s=dma(1), loss2_r=dma(1),
    loss3_s=dma(1), loss3_r=dma(1),
    core_s_s=dma(1), core_s_r=dma(N),
    zs_s=dma(1), zs_r=dma(5),
    plane_s=dma(1), big_s_r=dma(2, N), small_s_r=dma(2),
)
NAMES = list(SCRATCH)


class Refs:
    def __init__(self, refs):
        for name, ref in zip(NAMES, refs):
            setattr(self, name, ref)


def log_sum(parts):
    peak = parts[0]
    for part in parts[1:]:
        peak = jnp.maximum(peak, part)
    total = jnp.exp(parts[0] - peak)
    for part in parts[1:]:
        total = total + jnp.exp(part - peak)
    return peak + jnp.log(total)


def add(a, b):
    return (a.astype(F32) + b.astype(F32)).astype(BF16)


def kernel(img_hbm, txt_hbm, loss_out, both_out, *refs):
    s = Refs(refs)
    img, txt = lax.axis_index("img"), lax.axis_index("txt")
    y, zl = img // N, lax.rem(img, N)
    zh, xc = txt // (N * CORES), lax.rem(txt, N * CORES)
    x, c = xc // CORES, lax.rem(xc, CORES)
    z = zh * N + zl

    def up(place, by, count=N):
        return lax.rem(place + (by + count) % count, count)

    def at_x(place):
        return (img, (zh * N + place) * CORES + c)

    def at_xc(place):
        return (img, zh * (N * CORES) + place)

    def at_y(place):
        return (place * N + zl, txt)

    def at_z(place):
        return (y * N + lax.rem(place, N), (place // N) * (N * CORES) + xc)

    other_core = (img, (zh * N + x) * CORES + (1 - c))

    own_image = pltpu.make_async_copy(img_hbm, s.image.at[0], s.local_sem.at[0])
    own_text = pltpu.make_async_copy(txt_hbm.at[0], s.text.at[y, x, c], s.local_sem.at[1])
    own_image.start()
    own_text.start()

    barrier = pltpu.get_barrier_semaphore()
    partners = [at_z(up(z, by, NZ)) for by in (3, -3, 2, -2, 1, -1)]
    partners += [at_y(up(y, by)) for by in range(1, N)] + [at_x(up(x, by)) for by in range(1, N)]
    partners += [other_core]
    for partner in partners:
        pl.semaphore_signal(barrier, inc=1, device_id=partner, device_id_type=MESH)
    lane = lax.broadcasted_iota(jnp.int32, (8, COLS), 1)
    s.col_ids[...] = (
        zh * 4096 + lax.rem(lane // 64, 4) * 1024 + lax.rem(lane // 32, 2) * 512
        + (lane // 256) * 128 + zl * 32 + lax.rem(lane, 32)
    )
    pl.semaphore_wait(barrier, len(partners))


    def remote(src, dst, send_sem, recv_sem, device):
        return pltpu.make_async_remote_copy(
            src_ref=src, dst_ref=dst, send_sem=send_sem, recv_sem=recv_sem,
            device_id=device, device_id_type=MESH,
        )

    def send(*args):
        remote(*args).start()

    def wait_bytes(ref, sem):
        pltpu.make_async_copy(ref, ref, sem).wait()

    def exchange(buf, me, count, device, ss, rs):
        for by in sorted(range(1, count), key=lambda k: -min(k, count - k)):
            send(buf.at[me], buf.at[me], ss.at[0], rs.at[0], device(up(me, by, count)))

    def collect(buf, count, ss, rs):
        wait_bytes(buf.at[pl.ds(0, count - 1)], rs.at[0])
        wait_bytes(buf.at[pl.ds(0, count - 1)], ss.at[0])
        return [buf[j] for j in range(count)]

    class Gather:
        def __init__(self, slot, me, device, ss, rs):
            self.slot, self.me, self.device, self.ss, self.rs = slot, me, device, ss, rs

        def start(self):
            own = self.slot(self.me)
            for by in (2, 1, 3):
                send(own, own, self.ss, self.rs(by), self.device(up(self.me, by)))

        def wait(self, by):
            wait_bytes(self.slot(up(self.me, by)), self.rs(N - by))

    class Scatter:
        def __init__(self, slot, r, me, device, ss, rs):
            self.slot, self.r = slot, r
            self.me, self.device, self.ss, self.rs = me, device, ss, rs

        def start(self):
            for by in (2, 1, 3):
                to = up(self.me, by)
                send(self.slot(to), self.r.at[by], self.ss, self.rs, self.device(to))

        def finish(self):
            wait_bytes(self.r.at[pl.ds(1, 3)], self.rs)
            total = self.slot(self.me)[...].astype(F32)
            for by in (1, 3, 2):
                total = total + self.r[by].astype(F32)
            return total.astype(BF16)

    ends = [pl.ds(0, ROWS // 2), pl.ds(ROWS // 2, ROWS // 2)]

    def along(way, steps):
        return at_z(up(z, steps if way == 0 else -steps, NZ))

    def z_sem(way, reach):
        return s.zg_r.at[{3: way, 6: 2 + way, 1: 4, 2: 5, 4: 5}.get(reach, 6)]

    def slot(way, steps):
        return PLACES.index(steps if way == 1 or steps == FAR else -steps)

    def z_send(way, held, reaches):
        for reach in reaches:
            block, there = s.image.at[slot(way, held)], s.image.at[slot(way, reach)]
            if reach == FAR:
                block, there = block.at[ends[way]], there.at[ends[way]]
            send(block, there, s.zg_s.at[0], z_sem(way, reach), along(way, reach - held))

    halves = [pl.ds(0, WIDE), pl.ds(WIDE, WIDE)]
    small_g = [
        Gather(lambda o: s.text.at[y, o, c, :, halves[0]], x, at_x, s.text_s.at[0], lambda k: s.small_g_r.at[0, k]),
        Gather(lambda o: s.text.at[o, x, c, :, halves[1]], y, at_y, s.text_s.at[0], lambda k: s.small_g_r.at[1, k]),
    ]
    big_g = [
        [
            Gather(
                lambda o, q=up(x, by): s.text.at[o, q, c, :, halves[0]], y, at_y,
                s.text_s.at[0], lambda k, q=up(x, by): s.big_g_r.at[0, q],
            )
            for by in range(N)
        ],
        [
            Gather(
                lambda o, q=up(y, by): s.text.at[q, o, c, :, halves[1]], x, at_x,
                s.text_s.at[0], lambda k, q=up(y, by): s.big_g_r.at[1, q],
            )
            for by in range(N)
        ],
    ]

    def core_block(h, by, core):
        if h == 0:
            return s.text.at[:, up(x, by), core, :, halves[0]]
        return s.text.at[up(y, by), :, core, :, halves[1]]

    def share(by):
        for h in range(2):
            wait_bytes(s.line.at[h, pl.ds(0, 3)], s.big_g_r.at[h, up(x, by) if h == 0 else up(y, by)])
            block = core_block(h, by, c)
            send(block, block, s.core_g_s.at[0], s.core_g_r.at[0], other_core)

    own_image.wait()
    for reach in (3, 1):
        for way in range(2):
            z_send(way, 0, (reach,))
    own_text.wait()
    for h in range(2):
        small_g[h].start()
    for h in range(2):
        big_g[h][0].start()
    for by in (1, 3, 2):
        for h in range(2):
            small_g[h].wait(by)
            big_g[h][by].start()
    one = s.image.at[0]
    for way in range(2):
        wait_bytes(one, z_sem(way, 3))
        z_send(way, 3, (6, 4, 2))
    share(0)
    for way in range(2):
        wait_bytes(one, z_sem(way, 6))
        z_send(way, 6, (5, 7, 8))
    share(1)
    share(3)
    share(2)
    wait_bytes(s.image, s.core_g_r.at[0])

    row_place = lax.broadcasted_iota(jnp.int32, (STRIP, COLS), 0)

    def origin(g, strip):
        o = up(z, PLACES[g * N + strip], NZ)
        return o // N, lax.rem(o, N)

    def diagonal(g, strip):
        q, r = origin(g, strip)
        first = y * 4096 + r * 1024 + (q * N + x) * 64 + c * 32
        return row_place + first == s.col_ids[0:1, :]

    def in_lanes(g, strip):
        _, r = origin(g, strip)
        rows = lax.broadcasted_iota(jnp.int32, (STRIP, 128), 0)
        return rows + r * ROWS == lax.broadcasted_iota(jnp.int32, (STRIP, 128), 1)

    def in_rows(g, strip):
        q, _ = origin(g, strip)
        return lax.broadcasted_iota(jnp.int32, (N, 128), 0) == q

    s.row_dense[...] = jnp.zeros((N, 128), F32)
    s.diag[...] = jnp.zeros((8, 128), F32)

    def chunk_stats(q):
        images = s.image[q * N : (q + 1) * N].reshape(CHUNK, D)
        s.col_exp[q] = LOGIT_SCALE * lax.dot_general(
            images, s.text[...].reshape(COLS, D), (((1,), (1,)), ((), ())), preferred_element_type=F32
        )
        col_peak = None
        for strip in range(N):
            rows = slice(strip * STRIP, (strip + 1) * STRIP)
            logits = s.col_exp[q, rows, :]
            peak = jnp.max(logits, axis=1, keepdims=True)
            exps = jnp.exp(logits - peak)
            s.row_exp[q, rows, :] = exps
            s.row_peak[q, rows, :] = jnp.broadcast_to(peak, (STRIP, 128))
            log = peak + jnp.log(jnp.sum(exps, axis=1, keepdims=True))
            dense = jnp.sum(jnp.where(in_lanes(q, strip), log, 0.0), axis=0, keepdims=True)
            s.row_dense[...] += jnp.where(in_rows(q, strip), dense, 0.0)
            part = jnp.max(logits.reshape(STRIP // 8, 8, COLS), axis=0)
            col_peak = part if col_peak is None else jnp.maximum(col_peak, part)
        col_peak = jnp.max(col_peak, axis=0, keepdims=True)
        col_total = jnp.zeros((8, COLS), F32)
        diag = jnp.zeros((8, COLS), F32)
        for strip in range(N):
            rows = slice(strip * STRIP, (strip + 1) * STRIP)
            logits = s.col_exp[q, rows, :]
            exps = jnp.exp(logits - col_peak)
            s.col_exp[q, rows, :] = exps
            col_total = col_total + jnp.sum(exps.reshape(STRIP // 8, 8, COLS), axis=0)
            kept = jnp.where(diagonal(q, strip), logits, 0.0)
            diag = diag + jnp.sum(kept.reshape(STRIP // 8, 8, COLS), axis=0)
        s.diag[...] += sum(diag[:, j * 128 : (j + 1) * 128] for j in range(COLS // 128))
        s.col_peak[q] = jnp.broadcast_to(col_peak, (8, COLS))
        col_log = col_peak + jnp.log(jnp.sum(col_total, axis=0, keepdims=True))
        s.col_log[q] = jnp.broadcast_to(col_log, (8, COLS))

    wait_bytes(s.image.at[pl.ds(0, 2)], z_sem(0, 1))
    chunk_stats(0)
    wait_bytes(s.image.at[pl.ds(0, 4)], z_sem(0, 2))
    chunk_stats(1)
    wait_bytes(s.image.at[pl.ds(0, 5)], z_sem(0, 5))
    chunk_stats(2)
    chunk_stats(3)

    s.row1[z] = s.row_dense[...]
    exchange(s.row1, z, NZ, at_z, s.row1_s, s.row1_r)
    col_local = log_sum([s.col_log[j] for j in range(N)])[0:1]
    s.col1[xc] = jnp.concatenate([col_local[:, j * 128 : (j + 1) * 128] for j in range(8)], axis=0)
    exchange(s.col1, xc, N * CORES, at_xc, s.col1_s, s.col1_r)
    s.col2[y] = log_sum(collect(s.col1, N * CORES, s.col1_s, s.col1_r))
    exchange(s.col2, y, N, at_y, s.col2_s, s.col2_r)
    col_lse = log_sum(collect(s.col2, N, s.col2_s, s.col2_r))
    wide_col = jnp.concatenate([col_lse[j : j + 1] for j in range(8)], axis=1)
    row_lse = log_sum(collect(s.row1, NZ, s.row1_s, s.row1_r))
    for j in range(NZ):
        g, strip = j // N, j % N
        rows = slice(strip * STRIP, (strip + 1) * STRIP)
        lanes = jnp.sum(jnp.where(in_rows(g, strip), row_lse, 0.0), axis=0, keepdims=True)
        column = jnp.sum(jnp.where(in_lanes(g, strip), lanes, 0.0), axis=1, keepdims=True)
        s.row_scale[g, rows, :] = (0.5 * LOGIT_SCALE) * jnp.exp(s.row_peak[g, rows, :] - column)

    def chunk_weights(q):
        col_scale = (0.5 * LOGIT_SCALE) * jnp.exp(s.col_peak[q, 0:1, :] - wide_col)
        for strip in range(N):
            rows = slice(strip * STRIP, (strip + 1) * STRIP)
            row_scale = jnp.concatenate([s.row_scale[q, rows, :]] * (COLS // 128), axis=1)
            value = s.row_exp[q, rows, :] * row_scale + s.col_exp[q, rows, :] * col_scale
            value = value - jnp.where(diagonal(q, strip), LOGIT_SCALE, 0.0)
            s.weights[q, rows, :] = value.astype(BF16)

    for g in (3, 2, 1, 0):
        chunk_weights(g)

    def grad_image(g):
        out = jnp.dot(s.weights[g], s.text[...].reshape(COLS, D), preferred_element_type=F32)
        s.part_image[g * N : (g + 1) * N] = out.astype(BF16).reshape(N, ROWS, D)

    def z_part(way, steps):
        return s.part_image.at[slot(way, steps)]

    def zs_sem(way, steps):
        return s.zs_r.at[4 if steps in (1, 3) else (way if steps in (5, 7, 8) else 2 + way)]

    def z_give(steps, target):
        for way in range(2):
            block, there = z_part(way, steps), s.z_in.at[way, steps]
            if steps == FAR:
                block, there = block.at[ends[way]], there.at[ends[way]]
            send(block, there, s.zs_s.at[0], zs_sem(way, steps), along(way, -target))

    def z_hub(way, steps, parts):
        waited = s.image.at[pl.ds(0, 5), ends[0]] if FAR in parts else s.image.at[pl.ds(0, 3)]
        wait_bytes(waited, zs_sem(way, parts[0]))
        out = s.z_out.at[way, steps // 3 - 1]
        for p in range(2):
            total = z_part(way, steps)[ends[p]].astype(F32)
            for part in parts:
                if part != FAR or p == way:
                    total = total + s.z_in[way, part, ends[p]].astype(F32)
            out[ends[p]] = total.astype(BF16)
        send(out, s.z_in.at[way, steps], s.zs_s.at[0], zs_sem(way, steps), along(way, -3))

    def z_last():
        wait_bytes(s.image.at[pl.ds(0, 4)], zs_sem(0, 1))
        total = s.part_image[0].astype(F32)
        for steps in (1, 3):
            for way in range(2):
                total = total + s.z_in[way, steps].astype(F32)
        both_out[0] = total.astype(BF16)

    def grad_text(by):
        place = up(y, by)
        wide = N * CORES * ROWS
        columns = pl.ds(pl.multiple_of(place * wide, wide), wide)
        w = s.weights[:, :, columns].reshape(N * CHUNK, wide)
        out = lax.dot_general(
            w, s.image[...].reshape(NZ * ROWS, D), (((0,), (0,)), ((), ())), preferred_element_type=F32
        )
        s.part_text[place] = out.astype(BF16).reshape(N, CORES, ROWS, D)
        send(s.part_text.at[place, :, 1 - c], s.part_core.at[place], s.core_s_s.at[0], s.core_s_r.at[by], other_core)

    def add_core(by):
        place = up(y, by)
        wait_bytes(s.part_core.at[place], s.core_s_r.at[by])
        s.plane[place] = add(s.part_text[place, :, c], s.part_core[place])

    big_s = [
        [
            Scatter(
                lambda o, q=up(x, by): s.plane.at[o, q, :, halves[0]], s.big_in.at[0, up(x, by)], y, at_y,
                s.plane_s.at[0], s.big_s_r.at[0, up(x, by)],
            )
            for by in range(N)
        ],
        [
            Scatter(
                lambda o, q=up(y, by): s.plane.at[q, o, :, halves[1]], s.big_in.at[1, up(y, by)], x, at_x,
                s.plane_s.at[0], s.big_s_r.at[1, up(y, by)],
            )
            for by in range(N)
        ],
    ]
    small_s = [
        Scatter(lambda o: s.line.at[0, o], s.small_in.at[0], x, at_x, s.plane_s.at[0], s.small_s_r.at[0]),
        Scatter(lambda o: s.line.at[1, o], s.small_in.at[1], y, at_y, s.plane_s.at[0], s.small_s_r.at[1]),
    ]

    def fold(by):
        for h in range(2):
            q = up(x, by) if h == 0 else up(y, by)
            s.line[h, q] = big_s[h][by].finish()

    share_rows = jnp.sum(row_lse) * (1.0 / NZ)
    share_cols = jnp.sum(col_lse) * (1.0 / (N * N * CORES))
    own_share = share_rows + share_cols - 2.0 * jnp.sum(s.diag[...])
    s.loss3[z] = jnp.full((1, 128), own_share, F32)
    exchange(s.loss3, z, NZ, at_z, s.loss3_s, s.loss3_r)

    grad_image(3)
    z_give(8, 2)
    z_give(7, 1)
    grad_image(2)
    z_give(5, -1)
    grad_image(1)
    z_give(4, 1)
    z_give(2, -1)
    grad_image(0)
    for by in (2, 1, 3, 0):
        grad_text(by)
    z_give(1, 1)

    for by in (2, 1, 3, 0):
        add_core(by)
        big_s[1][by].start()
    for by in (2, 1, 3, 0):
        big_s[0][by].start()
    for way in range(2):
        z_hub(way, 6, (5, 7, 8))
    s.loss1[xc] = sum(collect(s.loss3, NZ, s.loss3_s, s.loss3_r))
    exchange(s.loss1, xc, N * CORES, at_xc, s.loss1_s, s.loss1_r)
    for by in (2, 1, 3, 0):
        fold(by)
    for h in range(2):
        small_s[h].start()
    for way in range(2):
        z_hub(way, 3, (2, 4, 6))
    s.loss2[y] = sum(collect(s.loss1, N * CORES, s.loss1_s, s.loss1_r))
    exchange(s.loss2, y, N, at_y, s.loss2_s, s.loss2_r)
    for h in range(2):
        both_out[1, :, halves[h]] = small_s[h].finish()
    total = sum(collect(s.loss2, N, s.loss2_s, s.loss2_r))
    loss_out[0, 0] = jnp.max(total) / (2.0 * PAIRS)
    z_last()

    fifteen = s.image.at[pl.ds(0, NZ - 1)]
    for sem in (s.zg_s, s.text_s, s.zs_s, s.plane_s):
        wait_bytes(fifteen, sem.at[0])
    for sem in (s.core_g_s, s.core_s_s):
        wait_bytes(s.image, sem.at[0])


def per_device(images, texts):
    loss, both = pl.pallas_call(
        kernel,
        out_shape=(
            jax.ShapeDtypeStruct((1, 1), F32),
            jax.ShapeDtypeStruct((2, ROWS, D), BF16),
        ),
        in_specs=[pl.BlockSpec(memory_space=pl.ANY)] * 2,
        out_specs=(
            pl.BlockSpec(memory_space=pltpu.SMEM),
            pl.BlockSpec(memory_space=pltpu.VMEM),
        ),
        scratch_shapes=list(SCRATCH.values()),
        compiler_params=pltpu.CompilerParams(
            collective_id=0, has_side_effects=True, vmem_limit_bytes=60 * 1024 * 1024
        ),
        name="contrastive",
    )(images, texts)
    return loss.reshape(()), both[0], both[1:2]


def solution(mesh):
    in_specs = (P(("img", "txt"), None), P("img", "txt", None))
    out_specs = (P(), P(("img", "txt"), None), P("img", "txt", None))
    return jax.shard_map(
        per_device, mesh=mesh, in_specs=in_specs, out_specs=out_specs, check_vma=False
    )
```

```python
import jax
import jax.numpy as jnp
from jax import lax
from jax.experimental import pallas as pl
from jax.experimental.pallas import tpu as pltpu
from jax.sharding import PartitionSpec as P

LOGIT_SCALE = 1.0 / 0.07
MESH = pl.DeviceIdType.MESH
F32 = jnp.float32
BF16 = jnp.bfloat16

N = 4
NZ = 16
CORES = 2
ROWS = 32
D = 1024
WIDE = D // 2
CHUNK = N * ROWS
COLS = N * N * CORES * ROWS
PAIRS = 16384
STRIP = ROWS
FAR = NZ // 2

PLACES = [0, 1, -1, 3, -3, 2, -2, 4, -4, 6, -6, 5, -5, 7, -7, 8]

def dma(*shape):
    return pltpu.SemaphoreType.DMA(shape)


def bf16(*shape):
    return pltpu.VMEM(shape, BF16)


def f32(*shape):
    return pltpu.VMEM(shape, F32)


SCRATCH = dict(
    image=bf16(NZ, ROWS, D),
    text=bf16(N, N, CORES, ROWS, D),
    row_exp=f32(N, CHUNK, COLS),
    col_exp=f32(N, CHUNK, COLS),
    row_peak=f32(N, CHUNK, 128),
    row_scale=f32(N, CHUNK, 128),
    row_dense=f32(N, 128),
    col_peak=f32(N, 8, COLS),
    col_log=f32(N, 8, COLS),
    col_ids=pltpu.VMEM((8, COLS), jnp.int32),
    diag=f32(8, 128),
    weights=bf16(N, CHUNK, COLS),
    part_image=bf16(NZ, ROWS, D),
    z_in=bf16(2, FAR + 1, ROWS, D),
    z_out=bf16(2, 2, ROWS, D),
    part_text=bf16(N, N, CORES, ROWS, D),
    part_core=bf16(N, N, ROWS, D),
    plane=bf16(N, N, ROWS, D),
    big_in=bf16(2, N, N, ROWS, WIDE),
    line=bf16(2, N, ROWS, WIDE),
    small_in=bf16(2, N, ROWS, WIDE),
    row1=f32(NZ, N, 128),
    col1=f32(N * CORES, 8, 128),
    col2=f32(N, 8, 128),
    loss1=f32(N * CORES, 1, 128),
    loss2=f32(N, 1, 128),
    loss3=f32(NZ, 1, 128),
    local_sem=dma(2),
    zg_s=dma(1), zg_r=dma(7),
    text_s=dma(1), small_g_r=dma(2, N), big_g_r=dma(2, N),
    core_g_s=dma(1), core_g_r=dma(1),
    row1_s=dma(1), row1_r=dma(1),
    col1_s=dma(1), col1_r=dma(1),
    col2_s=dma(1), col2_r=dma(1),
    loss1_s=dma(1), loss1_r=dma(1),
    loss2_s=dma(1), loss2_r=dma(1),
    loss3_s=dma(1), loss3_r=dma(1),
    core_s_s=dma(1), core_s_r=dma(N),
    zs_s=dma(1), zs_r=dma(5),
    plane_s=dma(1), big_s_r=dma(2, N), small_s_r=dma(2),
)
NAMES = list(SCRATCH)


class Refs:
    def __init__(self, refs):
        for name, ref in zip(NAMES, refs):
            setattr(self, name, ref)


def log_sum(parts):
    peak = parts[0]
    for part in parts[1:]:
        peak = jnp.maximum(peak, part)
    total = jnp.exp(parts[0] - peak)
    for part in parts[1:]:
        total = total + jnp.exp(part - peak)
    return peak + jnp.log(total)


def add(a, b):
    return (a.astype(F32) + b.astype(F32)).astype(BF16)


def kernel(img_hbm, txt_hbm, loss_out, both_out, *refs):
    s = Refs(refs)
    img, txt = lax.axis_index("img"), lax.axis_index("txt")
    y, zl = img // N, lax.rem(img, N)
    zh, xc = txt // (N * CORES), lax.rem(txt, N * CORES)
    x, c = xc // CORES, lax.rem(xc, CORES)
    z = zh * N + zl

    def up(place, by, count=N):
        return lax.rem(place + (by + count) % count, count)

    def at_x(place):
        return (img, (zh * N + place) * CORES + c)

    def at_xc(place):
        return (img, zh * (N * CORES) + place)

    def at_y(place):
        return (place * N + zl, txt)

    def at_z(place):
        return (y * N + lax.rem(place, N), (place // N) * (N * CORES) + xc)

    other_core = (img, (zh * N + x) * CORES + (1 - c))

    own_image = pltpu.make_async_copy(img_hbm, s.image.at[0], s.local_sem.at[0])
    own_text = pltpu.make_async_copy(txt_hbm.at[0], s.text.at[y, x, c], s.local_sem.at[1])
    own_image.start()
    own_text.start()

    barrier = pltpu.get_barrier_semaphore()
    partners = [at_z(up(z, by, NZ)) for by in (3, -3, 2, -2, 1, -1)]
    partners += [at_y(up(y, by)) for by in range(1, N)] + [at_x(up(x, by)) for by in range(1, N)]
    partners += [other_core]
    for partner in partners:
        pl.semaphore_signal(barrier, inc=1, device_id=partner, device_id_type=MESH)
    lane = lax.broadcasted_iota(jnp.int32, (8, COLS), 1)
    s.col_ids[...] = (
        zh * 4096 + lax.rem(lane // 64, 4) * 1024 + lax.rem(lane // 32, 2) * 512
        + (lane // 256) * 128 + zl * 32 + lax.rem(lane, 32)
    )
    pl.semaphore_wait(barrier, len(partners))


    def remote(src, dst, send_sem, recv_sem, device):
        return pltpu.make_async_remote_copy(
            src_ref=src, dst_ref=dst, send_sem=send_sem, recv_sem=recv_sem,
            device_id=device, device_id_type=MESH,
        )

    def send(*args):
        remote(*args).start()

    def wait_bytes(ref, sem):
        pltpu.make_async_copy(ref, ref, sem).wait()

    def exchange(buf, me, count, device, ss, rs):
        for by in sorted(range(1, count), key=lambda k: -min(k, count - k)):
            send(buf.at[me], buf.at[me], ss.at[0], rs.at[0], device(up(me, by, count)))

    def collect(buf, count, rs):
        wait_bytes(buf.at[pl.ds(0, count - 1)], rs.at[0])
        return [buf[j] for j in range(count)]

    class Gather:
        def __init__(self, slot, me, device, ss, rs):
            self.slot, self.me, self.device, self.ss, self.rs = slot, me, device, ss, rs

        def start(self):
            own = self.slot(self.me)
            for by in (2, 1, 3):
                send(own, own, self.ss, self.rs(by), self.device(up(self.me, by)))

        def wait(self, by):
            wait_bytes(self.slot(up(self.me, by)), self.rs(N - by))

    class Scatter:
        def __init__(self, slot, r, me, device, ss, rs):
            self.slot, self.r = slot, r
            self.me, self.device, self.ss, self.rs = me, device, ss, rs

        def start(self):
            for by in (2, 1, 3):
                to = up(self.me, by)
                send(self.slot(to), self.r.at[by], self.ss, self.rs, self.device(to))

        def finish(self):
            wait_bytes(self.r.at[pl.ds(1, 3)], self.rs)
            total = self.slot(self.me)[...].astype(F32)
            for by in (1, 3, 2):
                total = total + self.r[by].astype(F32)
            return total.astype(BF16)

    ends = [pl.ds(0, ROWS // 2), pl.ds(ROWS // 2, ROWS // 2)]

    def along(way, steps):
        return at_z(up(z, steps if way == 0 else -steps, NZ))

    def z_sem(way, reach):
        return s.zg_r.at[{3: way, 6: 2 + way, 1: 4, 2: 5, 4: 5}.get(reach, 6)]

    def slot(way, steps):
        return PLACES.index(steps if way == 1 or steps == FAR else -steps)

    def z_send(way, held, reaches):
        for reach in reaches:
            block, there = s.image.at[slot(way, held)], s.image.at[slot(way, reach)]
            if reach == FAR:
                block, there = block.at[ends[way]], there.at[ends[way]]
            send(block, there, s.zg_s.at[0], z_sem(way, reach), along(way, reach - held))

    halves = [pl.ds(0, WIDE), pl.ds(WIDE, WIDE)]
    small_g = [
        Gather(lambda o: s.text.at[y, o, c, :, halves[0]], x, at_x, s.text_s.at[0], lambda k: s.small_g_r.at[0, k]),
        Gather(lambda o: s.text.at[o, x, c, :, halves[1]], y, at_y, s.text_s.at[0], lambda k: s.small_g_r.at[1, k]),
    ]
    big_g = [
        [
            Gather(
                lambda o, q=up(x, by): s.text.at[o, q, c, :, halves[0]], y, at_y,
                s.text_s.at[0], lambda k, q=up(x, by): s.big_g_r.at[0, q],
            )
            for by in range(N)
        ],
        [
            Gather(
                lambda o, q=up(y, by): s.text.at[q, o, c, :, halves[1]], x, at_x,
                s.text_s.at[0], lambda k, q=up(y, by): s.big_g_r.at[1, q],
            )
            for by in range(N)
        ],
    ]

    def core_block(h, by, core):
        if h == 0:
            return s.text.at[:, up(x, by), core, :, halves[0]]
        return s.text.at[up(y, by), :, core, :, halves[1]]

    def share(by):
        for h in range(2):
            wait_bytes(s.line.at[h, pl.ds(0, 3)], s.big_g_r.at[h, up(x, by) if h == 0 else up(y, by)])
            block = core_block(h, by, c)
            send(block, block, s.core_g_s.at[0], s.core_g_r.at[0], other_core)

    own_image.wait()
    for reach in (3, 1):
        for way in range(2):
            z_send(way, 0, (reach,))
    own_text.wait()
    for h in range(2):
        small_g[h].start()
    for h in range(2):
        big_g[h][0].start()
    for by in (1, 3, 2):
        for h in range(2):
            small_g[h].wait(by)
            big_g[h][by].start()
    one = s.image.at[0]
    for way in range(2):
        wait_bytes(one, z_sem(way, 3))
        z_send(way, 3, (6, 4, 2))
    share(0)
    for way in range(2):
        wait_bytes(one, z_sem(way, 6))
        z_send(way, 6, (5, 7, 8))
    share(1)
    share(3)
    share(2)
    wait_bytes(s.image, s.core_g_r.at[0])

    row_place = lax.broadcasted_iota(jnp.int32, (STRIP, COLS), 0)

    def origin(g, strip):
        o = up(z, PLACES[g * N + strip], NZ)
        return o // N, lax.rem(o, N)

    def diagonal(g, strip):
        q, r = origin(g, strip)
        first = y * 4096 + r * 1024 + (q * N + x) * 64 + c * 32
        return row_place + first == s.col_ids[0:1, :]

    def in_lanes(g, strip):
        _, r = origin(g, strip)
        rows = lax.broadcasted_iota(jnp.int32, (STRIP, 128), 0)
        return rows + r * ROWS == lax.broadcasted_iota(jnp.int32, (STRIP, 128), 1)

    def in_rows(g, strip):
        q, _ = origin(g, strip)
        return lax.broadcasted_iota(jnp.int32, (N, 128), 0) == q

    s.row_dense[...] = jnp.zeros((N, 128), F32)
    s.diag[...] = jnp.zeros((8, 128), F32)

    def chunk_stats(q):
        images = s.image[q * N : (q + 1) * N].reshape(CHUNK, D)
        s.col_exp[q] = LOGIT_SCALE * lax.dot_general(
            images, s.text[...].reshape(COLS, D), (((1,), (1,)), ((), ())), preferred_element_type=F32
        )
        col_peak = None
        for strip in range(N):
            rows = slice(strip * STRIP, (strip + 1) * STRIP)
            logits = s.col_exp[q, rows, :]
            peak = jnp.max(logits, axis=1, keepdims=True)
            exps = jnp.exp(logits - peak)
            s.row_exp[q, rows, :] = exps
            s.row_peak[q, rows, :] = jnp.broadcast_to(peak, (STRIP, 128))
            log = peak + jnp.log(jnp.sum(exps, axis=1, keepdims=True))
            dense = jnp.sum(jnp.where(in_lanes(q, strip), log, 0.0), axis=0, keepdims=True)
            s.row_dense[...] += jnp.where(in_rows(q, strip), dense, 0.0)
            part = jnp.max(logits.reshape(STRIP // 8, 8, COLS), axis=0)
            col_peak = part if col_peak is None else jnp.maximum(col_peak, part)
        col_peak = jnp.max(col_peak, axis=0, keepdims=True)
        col_total = jnp.zeros((8, COLS), F32)
        diag = jnp.zeros((8, COLS), F32)
        for strip in range(N):
            rows = slice(strip * STRIP, (strip + 1) * STRIP)
            logits = s.col_exp[q, rows, :]
            exps = jnp.exp(logits - col_peak)
            s.col_exp[q, rows, :] = exps
            col_total = col_total + jnp.sum(exps.reshape(STRIP // 8, 8, COLS), axis=0)
            kept = jnp.where(diagonal(q, strip), logits, 0.0)
            diag = diag + jnp.sum(kept.reshape(STRIP // 8, 8, COLS), axis=0)
        s.diag[...] += sum(diag[:, j * 128 : (j + 1) * 128] for j in range(COLS // 128))
        s.col_peak[q] = jnp.broadcast_to(col_peak, (8, COLS))
        col_log = col_peak + jnp.log(jnp.sum(col_total, axis=0, keepdims=True))
        s.col_log[q] = jnp.broadcast_to(col_log, (8, COLS))

    wait_bytes(s.image.at[pl.ds(0, 2)], z_sem(0, 1))
    chunk_stats(0)
    wait_bytes(s.image.at[pl.ds(0, 4)], z_sem(0, 2))
    chunk_stats(1)
    wait_bytes(s.image.at[pl.ds(0, 5)], z_sem(0, 5))
    chunk_stats(2)
    chunk_stats(3)

    s.row1[z] = s.row_dense[...]
    exchange(s.row1, z, NZ, at_z, s.row1_s, s.row1_r)
    col_local = log_sum([s.col_log[j] for j in range(N)])[0:1]
    s.col1[xc] = jnp.concatenate([col_local[:, j * 128 : (j + 1) * 128] for j in range(8)], axis=0)
    exchange(s.col1, xc, N * CORES, at_xc, s.col1_s, s.col1_r)
    s.col2[y] = log_sum(collect(s.col1, N * CORES, s.col1_r))
    exchange(s.col2, y, N, at_y, s.col2_s, s.col2_r)
    col_lse = log_sum(collect(s.col2, N, s.col2_r))
    wide_col = jnp.concatenate([col_lse[j : j + 1] for j in range(8)], axis=1)
    row_lse = log_sum(collect(s.row1, NZ, s.row1_r))
    for j in range(NZ):
        g, strip = j // N, j % N
        rows = slice(strip * STRIP, (strip + 1) * STRIP)
        lanes = jnp.sum(jnp.where(in_rows(g, strip), row_lse, 0.0), axis=0, keepdims=True)
        column = jnp.sum(jnp.where(in_lanes(g, strip), lanes, 0.0), axis=1, keepdims=True)
        s.row_scale[g, rows, :] = (0.5 * LOGIT_SCALE) * jnp.exp(s.row_peak[g, rows, :] - column)

    def chunk_weights(q):
        col_scale = (0.5 * LOGIT_SCALE) * jnp.exp(s.col_peak[q, 0:1, :] - wide_col)
        for strip in range(N):
            rows = slice(strip * STRIP, (strip + 1) * STRIP)
            row_scale = jnp.concatenate([s.row_scale[q, rows, :]] * (COLS // 128), axis=1)
            value = s.row_exp[q, rows, :] * row_scale + s.col_exp[q, rows, :] * col_scale
            value = value - jnp.where(diagonal(q, strip), LOGIT_SCALE, 0.0)
            s.weights[q, rows, :] = value.astype(BF16)

    for g in (3, 2, 1, 0):
        chunk_weights(g)

    def grad_image(g):
        out = jnp.dot(s.weights[g], s.text[...].reshape(COLS, D), preferred_element_type=F32)
        s.part_image[g * N : (g + 1) * N] = out.astype(BF16).reshape(N, ROWS, D)

    def z_part(way, steps):
        return s.part_image.at[slot(way, steps)]

    def zs_sem(way, steps):
        return s.zs_r.at[4 if steps in (1, 3) else (way if steps in (5, 7, 8) else 2 + way)]

    def z_give(steps, target):
        for way in range(2):
            block, there = z_part(way, steps), s.z_in.at[way, steps]
            if steps == FAR:
                block, there = block.at[ends[way]], there.at[ends[way]]
            send(block, there, s.zs_s.at[0], zs_sem(way, steps), along(way, -target))

    def z_hub(way, steps, parts):
        waited = s.image.at[pl.ds(0, 5), ends[0]] if FAR in parts else s.image.at[pl.ds(0, 3)]
        wait_bytes(waited, zs_sem(way, parts[0]))
        out = s.z_out.at[way, steps // 3 - 1]
        for p in range(2):
            total = z_part(way, steps)[ends[p]].astype(F32)
            for part in parts:
                if part != FAR or p == way:
                    total = total + s.z_in[way, part, ends[p]].astype(F32)
            out[ends[p]] = total.astype(BF16)
        send(out, s.z_in.at[way, steps], s.zs_s.at[0], zs_sem(way, steps), along(way, -3))

    def z_last():
        wait_bytes(s.image.at[pl.ds(0, 4)], zs_sem(0, 1))
        total = s.part_image[0].astype(F32)
        for steps in (1, 3):
            for way in range(2):
                total = total + s.z_in[way, steps].astype(F32)
        both_out[0] = total.astype(BF16)

    def grad_text(by):
        place = up(y, by)
        wide = N * CORES * ROWS
        columns = pl.ds(pl.multiple_of(place * wide, wide), wide)
        w = s.weights[:, :, columns].reshape(N * CHUNK, wide)
        out = lax.dot_general(
            w, s.image[...].reshape(NZ * ROWS, D), (((0,), (0,)), ((), ())), preferred_element_type=F32
        )
        s.part_text[place] = out.astype(BF16).reshape(N, CORES, ROWS, D)
        send(s.part_text.at[place, :, 1 - c], s.part_core.at[place], s.core_s_s.at[0], s.core_s_r.at[by], other_core)

    def add_core(by):
        place = up(y, by)
        wait_bytes(s.part_core.at[place], s.core_s_r.at[by])
        s.plane[place] = add(s.part_text[place, :, c], s.part_core[place])

    big_s = [
        [
            Scatter(
                lambda o, q=up(x, by): s.plane.at[o, q, :, halves[0]], s.big_in.at[0, up(x, by)], y, at_y,
                s.plane_s.at[0], s.big_s_r.at[0, up(x, by)],
            )
            for by in range(N)
        ],
        [
            Scatter(
                lambda o, q=up(y, by): s.plane.at[q, o, :, halves[1]], s.big_in.at[1, up(y, by)], x, at_x,
                s.plane_s.at[0], s.big_s_r.at[1, up(y, by)],
            )
            for by in range(N)
        ],
    ]
    small_s = [
        Scatter(lambda o: s.line.at[0, o], s.small_in.at[0], x, at_x, s.plane_s.at[0], s.small_s_r.at[0]),
        Scatter(lambda o: s.line.at[1, o], s.small_in.at[1], y, at_y, s.plane_s.at[0], s.small_s_r.at[1]),
    ]

    def fold(by):
        for h in range(2):
            q = up(x, by) if h == 0 else up(y, by)
            s.line[h, q] = big_s[h][by].finish()

    share_rows = jnp.sum(row_lse) * (1.0 / NZ)
    share_cols = jnp.sum(col_lse) * (1.0 / (N * N * CORES))
    own_share = share_rows + share_cols - 2.0 * jnp.sum(s.diag[...])
    s.loss3[z] = jnp.full((1, 128), own_share, F32)
    exchange(s.loss3, z, NZ, at_z, s.loss3_s, s.loss3_r)

    grad_image(3)
    z_give(8, 2)
    z_give(7, 1)
    grad_image(2)
    z_give(5, -1)
    grad_image(1)
    z_give(4, 1)
    z_give(2, -1)
    grad_image(0)
    for by in (2, 1, 3, 0):
        grad_text(by)
    z_give(1, 1)

    for by in (2, 1, 3, 0):
        add_core(by)
        big_s[1][by].start()
    for by in (2, 1, 3, 0):
        big_s[0][by].start()
    for way in range(2):
        z_hub(way, 6, (5, 7, 8))
    s.loss1[xc] = sum(collect(s.loss3, NZ, s.loss3_r))
    exchange(s.loss1, xc, N * CORES, at_xc, s.loss1_s, s.loss1_r)
    for by in (2, 1, 3, 0):
        fold(by)
    for h in range(2):
        small_s[h].start()
    for way in range(2):
        z_hub(way, 3, (2, 4, 6))
    s.loss2[y] = sum(collect(s.loss1, N * CORES, s.loss1_r))
    exchange(s.loss2, y, N, at_y, s.loss2_s, s.loss2_r)
    for h in range(2):
        both_out[1, :, halves[h]] = small_s[h].finish()
    total = sum(collect(s.loss2, N, s.loss2_r))
    loss_out[0, 0] = jnp.max(total) / (2.0 * PAIRS)
    z_last()

    tiles = ((s.row1, s.row1_s), (s.col1, s.col1_s), (s.col2, s.col2_s))
    tiles += ((s.loss1, s.loss1_s), (s.loss2, s.loss2_s), (s.loss3, s.loss3_s))
    for buf, sem in tiles:
        wait_bytes(buf.at[pl.ds(0, buf.shape[0] - 1)], sem.at[0])
    fifteen = s.image.at[pl.ds(0, NZ - 1)]
    for sem in (s.zg_s, s.text_s, s.zs_s, s.plane_s):
        wait_bytes(fifteen, sem.at[0])
    for sem in (s.core_g_s, s.core_s_s):
        wait_bytes(s.image, sem.at[0])


def per_device(images, texts):
    loss, both = pl.pallas_call(
        kernel,
        out_shape=(
            jax.ShapeDtypeStruct((1, 1), F32),
            jax.ShapeDtypeStruct((2, ROWS, D), BF16),
        ),
        in_specs=[pl.BlockSpec(memory_space=pl.ANY)] * 2,
        out_specs=(
            pl.BlockSpec(memory_space=pltpu.SMEM),
            pl.BlockSpec(memory_space=pltpu.VMEM),
        ),
        scratch_shapes=list(SCRATCH.values()),
        compiler_params=pltpu.CompilerParams(
            collective_id=0, has_side_effects=True, vmem_limit_bytes=60 * 1024 * 1024
        ),
        name="contrastive",
    )(images, texts)
    return loss.reshape(()), both[0], both[1:2]


def solution(mesh):
    in_specs = (P(("img", "txt"), None), P("img", "txt", None))
    out_specs = (P(), P(("img", "txt"), None), P("img", "txt", None))
    return jax.shard_map(
        per_device, mesh=mesh, in_specs=in_specs, out_specs=out_specs, check_vma=False
    )
```

```python
import jax
import jax.numpy as jnp
from jax import lax
from jax.experimental import pallas as pl
from jax.experimental.pallas import tpu as pltpu
from jax.sharding import PartitionSpec as P

LOGIT_SCALE = 1.0 / 0.07
MESH = pl.DeviceIdType.MESH
F32 = jnp.float32
BF16 = jnp.bfloat16

N = 4
NZ = 16
CORES = 2
ROWS = 32
D = 1024
WIDE = D // 2
CHUNK = N * ROWS
COLS = N * N * CORES * ROWS
PAIRS = 16384
STRIP = ROWS
FAR = NZ // 2

PLACES = [0, 1, -1, 3, -3, 2, -2, 4, -4, 6, -6, 5, -5, 7, -7, 8]

def dma(*shape):
    return pltpu.SemaphoreType.DMA(shape)


def bf16(*shape):
    return pltpu.VMEM(shape, BF16)


def f32(*shape):
    return pltpu.VMEM(shape, F32)


SCRATCH = dict(
    image=bf16(NZ, ROWS, D),
    text=bf16(N, N, CORES, ROWS, D),
    row_exp=f32(N, CHUNK, COLS),
    col_exp=f32(N, CHUNK, COLS),
    row_peak=f32(N, CHUNK, 128),
    row_scale=f32(N, CHUNK, 128),
    row_dense=f32(N, 128),
    col_peak=f32(N, 8, COLS),
    col_log=f32(N, 8, COLS),
    col_ids=pltpu.VMEM((8, COLS), jnp.int32),
    diag=f32(8, 128),
    weights=bf16(N, CHUNK, COLS),
    part_image=bf16(NZ, ROWS, D),
    z_in=bf16(2, FAR + 1, ROWS, D),
    z_out=bf16(2, 2, ROWS, D),
    part_text=bf16(N, N, CORES, ROWS, D),
    part_core=bf16(N, N, ROWS, D),
    plane=bf16(N, N, ROWS, D),
    big_in=bf16(2, N, N, ROWS, WIDE),
    line=bf16(2, N, ROWS, WIDE),
    small_in=bf16(2, N, ROWS, WIDE),
    row1=f32(NZ, N, 128),
    col1=f32(N * CORES, 8, 128),
    col2=f32(N, 8, 128),
    loss1=f32(N * CORES, 1, 128),
    loss2=f32(N, 1, 128),
    loss3=f32(NZ, 1, 128),
    local_sem=dma(2),
    zg_s=dma(1), zg_r=dma(7),
    text_s=dma(1), small_g_r=dma(2, N), big_g_r=dma(2, N),
    core_g_s=dma(1), core_g_r=dma(1),
    row1_s=dma(1), row1_r=dma(1),
    col1_s=dma(1), col1_r=dma(1),
    col2_s=dma(1), col2_r=dma(1),
    loss1_s=dma(1), loss1_r=dma(1),
    loss2_s=dma(1), loss2_r=dma(1),
    loss3_s=dma(1), loss3_r=dma(1),
    core_s_s=dma(1), core_s_r=dma(N),
    zs_s=dma(1), zs_r=dma(5),
    plane_s=dma(1), big_s_r=dma(2, N), small_s_r=dma(2),
)
NAMES = list(SCRATCH)


class Refs:
    def __init__(self, refs):
        for name, ref in zip(NAMES, refs):
            setattr(self, name, ref)


def log_sum(parts):
    peak = parts[0]
    for part in parts[1:]:
        peak = jnp.maximum(peak, part)
    total = jnp.exp(parts[0] - peak)
    for part in parts[1:]:
        total = total + jnp.exp(part - peak)
    return peak + jnp.log(total)


def add(a, b):
    return (a.astype(F32) + b.astype(F32)).astype(BF16)


def kernel(img_hbm, txt_hbm, loss_out, both_out, *refs):
    s = Refs(refs)
    img, txt = lax.axis_index("img"), lax.axis_index("txt")
    y, zl = img // N, lax.rem(img, N)
    zh, xc = txt // (N * CORES), lax.rem(txt, N * CORES)
    x, c = xc // CORES, lax.rem(xc, CORES)
    z = zh * N + zl

    def up(place, by, count=N):
        return lax.rem(place + (by + count) % count, count)

    def at_x(place):
        return (img, (zh * N + place) * CORES + c)

    def at_xc(place):
        return (img, zh * (N * CORES) + place)

    def at_y(place):
        return (place * N + zl, txt)

    def at_z(place):
        return (y * N + lax.rem(place, N), (place // N) * (N * CORES) + xc)

    other_core = (img, (zh * N + x) * CORES + (1 - c))

    own_image = pltpu.make_async_copy(img_hbm, s.image.at[0], s.local_sem.at[0])
    own_text = pltpu.make_async_copy(txt_hbm.at[0], s.text.at[y, x, c], s.local_sem.at[1])
    own_image.start()
    own_text.start()

    barrier = pltpu.get_barrier_semaphore()
    partners = [at_z(up(z, by, NZ)) for by in (3, -3, 2, -2, 1, -1)]
    partners += [at_y(up(y, by)) for by in range(1, N)] + [at_x(up(x, by)) for by in range(1, N)]
    partners += [other_core]
    for partner in partners:
        pl.semaphore_signal(barrier, inc=1, device_id=partner, device_id_type=MESH)
    lane = lax.broadcasted_iota(jnp.int32, (8, COLS), 1)
    s.col_ids[...] = (
        zh * 4096 + lax.rem(lane // 64, 4) * 1024 + lax.rem(lane // 32, 2) * 512
        + (lane // 256) * 128 + zl * 32 + lax.rem(lane, 32)
    )
    pl.semaphore_wait(barrier, len(partners))


    def remote(src, dst, send_sem, recv_sem, device):
        return pltpu.make_async_remote_copy(
            src_ref=src, dst_ref=dst, send_sem=send_sem, recv_sem=recv_sem,
            device_id=device, device_id_type=MESH,
        )

    def send(*args):
        remote(*args).start()

    def wait_bytes(ref, sem):
        pltpu.make_async_copy(ref, ref, sem).wait()

    def exchange(buf, me, count, device, ss, rs):
        for by in sorted(range(1, count), key=lambda k: -min(k, count - k)):
            send(buf.at[me], buf.at[me], ss.at[0], rs.at[0], device(up(me, by, count)))

    def collect(buf, count, rs):
        wait_bytes(buf.at[pl.ds(0, count - 1)], rs.at[0])
        return [buf[j] for j in range(count)]

    class Gather:
        def __init__(self, slot, me, device, ss, rs):
            self.slot, self.me, self.device, self.ss, self.rs = slot, me, device, ss, rs

        def start(self):
            own = self.slot(self.me)
            for by in (2, 1, 3):
                send(own, own, self.ss, self.rs(by), self.device(up(self.me, by)))

        def wait(self, by):
            wait_bytes(self.slot(up(self.me, by)), self.rs(N - by))

    class Scatter:
        def __init__(self, slot, r, me, device, ss, rs):
            self.slot, self.r = slot, r
            self.me, self.device, self.ss, self.rs = me, device, ss, rs

        def start(self):
            for by in (2, 1, 3):
                to = up(self.me, by)
                send(self.slot(to), self.r.at[by], self.ss, self.rs, self.device(to))

        def finish(self):
            wait_bytes(self.r.at[pl.ds(1, 3)], self.rs)
            total = self.slot(self.me)[...].astype(F32)
            for by in (1, 3, 2):
                total = total + self.r[by].astype(F32)
            return total.astype(BF16)

    ends = [pl.ds(0, ROWS // 2), pl.ds(ROWS // 2, ROWS // 2)]

    def along(way, steps):
        return at_z(up(z, steps if way == 0 else -steps, NZ))

    def z_sem(way, reach):
        return s.zg_r.at[{3: way, 6: 2 + way, 1: 4, 2: 5, 4: 5}.get(reach, 6)]

    def slot(way, steps):
        return PLACES.index(steps if way == 1 or steps == FAR else -steps)

    def z_send(way, held, reaches):
        for reach in reaches:
            block, there = s.image.at[slot(way, held)], s.image.at[slot(way, reach)]
            if reach == FAR:
                block, there = block.at[ends[way]], there.at[ends[way]]
            send(block, there, s.zg_s.at[0], z_sem(way, reach), along(way, reach - held))

    halves = [pl.ds(0, WIDE), pl.ds(WIDE, WIDE)]
    small_g = [
        Gather(lambda o: s.text.at[y, o, c, :, halves[0]], x, at_x, s.text_s.at[0], lambda k: s.small_g_r.at[0, k]),
        Gather(lambda o: s.text.at[o, x, c, :, halves[1]], y, at_y, s.text_s.at[0], lambda k: s.small_g_r.at[1, k]),
    ]
    big_g = [
        [
            Gather(
                lambda o, q=up(x, by): s.text.at[o, q, c, :, halves[0]], y, at_y,
                s.text_s.at[0], lambda k, q=up(x, by): s.big_g_r.at[0, q],
            )
            for by in range(N)
        ],
        [
            Gather(
                lambda o, q=up(y, by): s.text.at[q, o, c, :, halves[1]], x, at_x,
                s.text_s.at[0], lambda k, q=up(y, by): s.big_g_r.at[1, q],
            )
            for by in range(N)
        ],
    ]

    def core_block(h, by, core):
        if h == 0:
            return s.text.at[:, up(x, by), core, :, halves[0]]
        return s.text.at[up(y, by), :, core, :, halves[1]]

    def share(by):
        for h in range(2):
            wait_bytes(s.line.at[h, pl.ds(0, 3)], s.big_g_r.at[h, up(x, by) if h == 0 else up(y, by)])
            block = core_block(h, by, c)
            send(block, block, s.core_g_s.at[0], s.core_g_r.at[0], other_core)

    own_image.wait()
    for reach in (3, 1):
        for way in range(2):
            z_send(way, 0, (reach,))
    own_text.wait()
    for h in range(2):
        small_g[h].start()
    for h in range(2):
        big_g[h][0].start()
    for by in (1, 3, 2):
        for h in range(2):
            small_g[h].wait(by)
            big_g[h][by].start()
    one = s.image.at[0]
    for way in range(2):
        wait_bytes(one, z_sem(way, 3))
        z_send(way, 3, (6, 4, 2))
    share(0)
    for way in range(2):
        wait_bytes(one, z_sem(way, 6))
        z_send(way, 6, (5, 7, 8))
    share(1)
    share(3)
    share(2)
    wait_bytes(s.image, s.core_g_r.at[0])

    row_place = lax.broadcasted_iota(jnp.int32, (STRIP, COLS), 0)

    def origin(g, strip):
        o = up(z, PLACES[g * N + strip], NZ)
        return o // N, lax.rem(o, N)

    def diagonal(g, strip):
        q, r = origin(g, strip)
        first = y * 4096 + r * 1024 + (q * N + x) * 64 + c * 32
        return row_place + first == s.col_ids[0:1, :]

    def in_lanes(g, strip):
        _, r = origin(g, strip)
        rows = lax.broadcasted_iota(jnp.int32, (STRIP, 128), 0)
        return rows + r * ROWS == lax.broadcasted_iota(jnp.int32, (STRIP, 128), 1)

    def in_rows(g, strip):
        q, _ = origin(g, strip)
        return lax.broadcasted_iota(jnp.int32, (N, 128), 0) == q

    s.row_dense[...] = jnp.zeros((N, 128), F32)
    s.diag[...] = jnp.zeros((8, 128), F32)

    def chunk_stats(q):
        images = s.image[q * N : (q + 1) * N].reshape(CHUNK, D)
        s.col_exp[q] = LOGIT_SCALE * lax.dot_general(
            images, s.text[...].reshape(COLS, D), (((1,), (1,)), ((), ())), preferred_element_type=F32
        )
        col_peak = None
        for strip in range(N):
            rows = slice(strip * STRIP, (strip + 1) * STRIP)
            logits = s.col_exp[q, rows, :]
            peak = jnp.max(logits, axis=1, keepdims=True)
            exps = jnp.exp(logits - peak)
            s.row_exp[q, rows, :] = exps
            s.row_peak[q, rows, :] = jnp.broadcast_to(peak, (STRIP, 128))
            log = peak + jnp.log(jnp.sum(exps, axis=1, keepdims=True))
            dense = jnp.sum(jnp.where(in_lanes(q, strip), log, 0.0), axis=0, keepdims=True)
            s.row_dense[...] += jnp.where(in_rows(q, strip), dense, 0.0)
            part = jnp.max(logits.reshape(STRIP // 8, 8, COLS), axis=0)
            col_peak = part if col_peak is None else jnp.maximum(col_peak, part)
        col_peak = jnp.max(col_peak, axis=0, keepdims=True)
        col_total = jnp.zeros((8, COLS), F32)
        diag = jnp.zeros((8, COLS), F32)
        for strip in range(N):
            rows = slice(strip * STRIP, (strip + 1) * STRIP)
            logits = s.col_exp[q, rows, :]
            exps = jnp.exp(logits - col_peak)
            s.col_exp[q, rows, :] = exps
            col_total = col_total + jnp.sum(exps.reshape(STRIP // 8, 8, COLS), axis=0)
            kept = jnp.where(diagonal(q, strip), logits, 0.0)
            diag = diag + jnp.sum(kept.reshape(STRIP // 8, 8, COLS), axis=0)
        s.diag[...] += sum(diag[:, j * 128 : (j + 1) * 128] for j in range(COLS // 128))
        s.col_peak[q] = jnp.broadcast_to(col_peak, (8, COLS))
        col_log = col_peak + jnp.log(jnp.sum(col_total, axis=0, keepdims=True))
        s.col_log[q] = jnp.broadcast_to(col_log, (8, COLS))

    wait_bytes(s.image.at[pl.ds(0, 2)], z_sem(0, 1))
    chunk_stats(0)
    wait_bytes(s.image.at[pl.ds(0, 4)], z_sem(0, 2))
    chunk_stats(1)
    wait_bytes(s.image.at[pl.ds(0, 5)], z_sem(0, 5))
    chunk_stats(2)
    chunk_stats(3)

    s.row1[z] = s.row_dense[...]
    exchange(s.row1, z, NZ, at_z, s.row1_s, s.row1_r)
    col_local = log_sum([s.col_log[j] for j in range(N)])[0:1]
    s.col1[xc] = jnp.concatenate([col_local[:, j * 128 : (j + 1) * 128] for j in range(8)], axis=0)
    exchange(s.col1, xc, N * CORES, at_xc, s.col1_s, s.col1_r)
    s.col2[y] = log_sum(collect(s.col1, N * CORES, s.col1_r))
    exchange(s.col2, y, N, at_y, s.col2_s, s.col2_r)
    col_lse = log_sum(collect(s.col2, N, s.col2_r))
    wide_col = jnp.concatenate([col_lse[j : j + 1] for j in range(8)], axis=1)
    row_lse = log_sum(collect(s.row1, NZ, s.row1_r))
    for j in range(NZ):
        g, strip = j // N, j % N
        rows = slice(strip * STRIP, (strip + 1) * STRIP)
        lanes = jnp.sum(jnp.where(in_rows(g, strip), row_lse, 0.0), axis=0, keepdims=True)
        column = jnp.sum(jnp.where(in_lanes(g, strip), lanes, 0.0), axis=1, keepdims=True)
        s.row_scale[g, rows, :] = (0.5 * LOGIT_SCALE) * jnp.exp(s.row_peak[g, rows, :] - column)
    share_rows = jnp.sum(row_lse) * (1.0 / NZ)
    share_cols = jnp.sum(col_lse) * (1.0 / (N * N * CORES))
    own_share = share_rows + share_cols - 2.0 * jnp.sum(s.diag[...])
    s.loss3[z] = jnp.full((1, 128), own_share, F32)
    exchange(s.loss3, z, NZ, at_z, s.loss3_s, s.loss3_r)


    def chunk_weights(q):
        col_scale = (0.5 * LOGIT_SCALE) * jnp.exp(s.col_peak[q, 0:1, :] - wide_col)
        for strip in range(N):
            rows = slice(strip * STRIP, (strip + 1) * STRIP)
            row_scale = jnp.concatenate([s.row_scale[q, rows, :]] * (COLS // 128), axis=1)
            value = s.row_exp[q, rows, :] * row_scale + s.col_exp[q, rows, :] * col_scale
            value = value - jnp.where(diagonal(q, strip), LOGIT_SCALE, 0.0)
            s.weights[q, rows, :] = value.astype(BF16)

    for g in (3, 2, 1, 0):
        chunk_weights(g)

    def grad_image(g):
        out = jnp.dot(s.weights[g], s.text[...].reshape(COLS, D), preferred_element_type=F32)
        s.part_image[g * N : (g + 1) * N] = out.astype(BF16).reshape(N, ROWS, D)

    def z_part(way, steps):
        return s.part_image.at[slot(way, steps)]

    def zs_sem(way, steps):
        return s.zs_r.at[4 if steps in (1, 3) else (way if steps in (5, 7, 8) else 2 + way)]

    def z_give(steps, target):
        for way in range(2):
            block, there = z_part(way, steps), s.z_in.at[way, steps]
            if steps == FAR:
                block, there = block.at[ends[way]], there.at[ends[way]]
            send(block, there, s.zs_s.at[0], zs_sem(way, steps), along(way, -target))

    def z_hub(way, steps, parts):
        waited = s.image.at[pl.ds(0, 5), ends[0]] if FAR in parts else s.image.at[pl.ds(0, 3)]
        wait_bytes(waited, zs_sem(way, parts[0]))
        out = s.z_out.at[way, steps // 3 - 1]
        for p in range(2):
            total = z_part(way, steps)[ends[p]].astype(F32)
            for part in parts:
                if part != FAR or p == way:
                    total = total + s.z_in[way, part, ends[p]].astype(F32)
            out[ends[p]] = total.astype(BF16)
        send(out, s.z_in.at[way, steps], s.zs_s.at[0], zs_sem(way, steps), along(way, -3))

    def z_last():
        wait_bytes(s.image.at[pl.ds(0, 4)], zs_sem(0, 1))
        total = s.part_image[0].astype(F32)
        for steps in (1, 3):
            for way in range(2):
                total = total + s.z_in[way, steps].astype(F32)
        both_out[0] = total.astype(BF16)

    def grad_text(by):
        place = up(y, by)
        wide = N * CORES * ROWS
        columns = pl.ds(pl.multiple_of(place * wide, wide), wide)
        w = s.weights[:, :, columns].reshape(N * CHUNK, wide)
        out = lax.dot_general(
            w, s.image[...].reshape(NZ * ROWS, D), (((0,), (0,)), ((), ())), preferred_element_type=F32
        )
        s.part_text[place] = out.astype(BF16).reshape(N, CORES, ROWS, D)
        send(s.part_text.at[place, :, 1 - c], s.part_core.at[place], s.core_s_s.at[0], s.core_s_r.at[by], other_core)

    def add_core(by):
        place = up(y, by)
        wait_bytes(s.part_core.at[place], s.core_s_r.at[by])
        s.plane[place] = add(s.part_text[place, :, c], s.part_core[place])

    big_s = [
        [
            Scatter(
                lambda o, q=up(x, by): s.plane.at[o, q, :, halves[0]], s.big_in.at[0, up(x, by)], y, at_y,
                s.plane_s.at[0], s.big_s_r.at[0, up(x, by)],
            )
            for by in range(N)
        ],
        [
            Scatter(
                lambda o, q=up(y, by): s.plane.at[q, o, :, halves[1]], s.big_in.at[1, up(y, by)], x, at_x,
                s.plane_s.at[0], s.big_s_r.at[1, up(y, by)],
            )
            for by in range(N)
        ],
    ]
    small_s = [
        Scatter(lambda o: s.line.at[0, o], s.small_in.at[0], x, at_x, s.plane_s.at[0], s.small_s_r.at[0]),
        Scatter(lambda o: s.line.at[1, o], s.small_in.at[1], y, at_y, s.plane_s.at[0], s.small_s_r.at[1]),
    ]

    def fold(by):
        for h in range(2):
            q = up(x, by) if h == 0 else up(y, by)
            s.line[h, q] = big_s[h][by].finish()

    grad_image(3)
    z_give(8, 2)
    z_give(7, 1)
    grad_image(2)
    z_give(5, -1)
    grad_image(1)
    z_give(4, 1)
    z_give(2, -1)
    grad_image(0)
    for by in (2, 1, 3, 0):
        grad_text(by)
    z_give(1, 1)

    for by in (2, 1, 3, 0):
        add_core(by)
        big_s[1][by].start()
    for by in (2, 1, 3, 0):
        big_s[0][by].start()
    for way in range(2):
        z_hub(way, 6, (5, 7, 8))
    s.loss1[xc] = sum(collect(s.loss3, NZ, s.loss3_r))
    exchange(s.loss1, xc, N * CORES, at_xc, s.loss1_s, s.loss1_r)
    for by in (2, 1, 3, 0):
        fold(by)
    for h in range(2):
        small_s[h].start()
    for way in range(2):
        z_hub(way, 3, (2, 4, 6))
    s.loss2[y] = sum(collect(s.loss1, N * CORES, s.loss1_r))
    exchange(s.loss2, y, N, at_y, s.loss2_s, s.loss2_r)
    for h in range(2):
        both_out[1, :, halves[h]] = small_s[h].finish()
    total = sum(collect(s.loss2, N, s.loss2_r))
    loss_out[0, 0] = jnp.max(total) / (2.0 * PAIRS)
    z_last()

    tiles = ((s.row1, s.row1_s), (s.col1, s.col1_s), (s.col2, s.col2_s))
    tiles += ((s.loss1, s.loss1_s), (s.loss2, s.loss2_s), (s.loss3, s.loss3_s))
    for buf, sem in tiles:
        wait_bytes(buf.at[pl.ds(0, buf.shape[0] - 1)], sem.at[0])
    fifteen = s.image.at[pl.ds(0, NZ - 1)]
    for sem in (s.zg_s, s.text_s, s.zs_s, s.plane_s):
        wait_bytes(fifteen, sem.at[0])
    for sem in (s.core_g_s, s.core_s_s):
        wait_bytes(s.image, sem.at[0])


def per_device(images, texts):
    loss, both = pl.pallas_call(
        kernel,
        out_shape=(
            jax.ShapeDtypeStruct((1, 1), F32),
            jax.ShapeDtypeStruct((2, ROWS, D), BF16),
        ),
        in_specs=[pl.BlockSpec(memory_space=pl.ANY)] * 2,
        out_specs=(
            pl.BlockSpec(memory_space=pltpu.SMEM),
            pl.BlockSpec(memory_space=pltpu.VMEM),
        ),
        scratch_shapes=list(SCRATCH.values()),
        compiler_params=pltpu.CompilerParams(
            collective_id=0, has_side_effects=True, vmem_limit_bytes=60 * 1024 * 1024
        ),
        name="contrastive",
    )(images, texts)
    return loss.reshape(()), both[0], both[1:2]


def solution(mesh):
    in_specs = (P(("img", "txt"), None), P("img", "txt", None))
    out_specs = (P(), P(("img", "txt"), None), P("img", "txt", None))
    return jax.shard_map(
        per_device, mesh=mesh, in_specs=in_specs, out_specs=out_specs, check_vma=False
    )
```
